128 devices in a mesh: lon: 8 (over y, core), lat: 16 (over z, x).
Axes of the slice: x: 4, y: 4, z: 4, core: 2. Of those that a mesh axis runs over, the one named last changes fastest.
Arguments:
- state: float32 [512, 4, 16, 2880], P('lat', None, None, 'lon'), may hold values from -6 to 6
- band: int32 [256], replicated, may hold values from 1 to 32, as said below
- damping: float32 [256], replicated, may hold values from 0.2 to 0.9
Outputs:
- advanced: float32 [512, 4, 16, 2880], P('lat', None, None, 'lon')
The draws below stay inside these ranges and needn't reach their ends.
Inputs may be any that keep to these rules, and one draw needn't show every extreme that they name: Each polar latitude's band half width is an integer from 1 to 32; 32 is reached at some latitude.
All inputs are finite; a program needn't handle non-finite values.
Results may differ from the reference program's by a relative error of at most 0.00007.
Values sent between devices are 32-bit elements; how exact they have to be, the bound alone decides.
A program may use at most 128 MiB of HBM per device.

```python
import math
import jax
import jax.numpy as jnp
from jax import lax

NLON = 2880
NF = 4
MAXB = 32
LEV = 16
NLAT = 512
PLAT = 256


def draw_band(key, part):
    first_key = jax.random.fold_in(key, 11)
    second_key = jax.random.fold_in(key, 12)
    values = jax.random.randint(first_key, (PLAT,), 1, MAXB + 1)
    widest = jax.random.randint(second_key, (), 0, PLAT)
    return jnp.where(jnp.arange(PLAT) == widest, MAXB, values).astype(jnp.int32)


def block_levels(key, shape, cuts, smallest, top_value):
    gain, own = 1.0, jax.random.fold_in(key, 6)
    for dim, parts in cuts:
        heights = jnp.exp(jax.random.uniform(jax.random.fold_in(own, dim), (parts,), jnp.float32, smallest / len(cuts), top_value / len(cuts)))
        gain = gain * jnp.repeat(heights, shape[dim] // parts).reshape([-1 if axis == dim else 1 for axis in range(len(shape))])
    return gain


def gaussian(own_key, shape, spread, reach, shards=(), dtype=jnp.bfloat16):
    entries = jax.random.normal(own_key, shape, jnp.float32) * spread
    if len(shards) > 0:
        entries = block_levels(own_key, shape, shards, -0.22, 0.18) * entries
    return jnp.clip(entries, min=-reach, max=reach).astype(dtype)


def setup_inputs(seed: int = 0) -> dict:
    key_of = jax.random.split(jax.random.key(seed), 4)
    return {
        "state": gaussian(key_of[0], (NLAT, NF, LEV, NLON), 1.0, 6.0, ((0, 16), (3, 8)), jnp.float32),
        "band": draw_band(jax.random.fold_in(key_of[3], 71), 0),
        "damping": jnp.clip(jnp.exp(jax.random.uniform(key_of[2], (PLAT,), jnp.float32, math.log(0.2), math.log(0.9))), 0.2, 0.9),
    }


KX = 0.004
KY = 0.1
FC = 0.2


def advance_cells(padded, cos_rows, sin_rows, cos_pad):
    u = padded[:, 0]
    v = padded[:, 1]
    h = padded[:, 2]
    q = padded[:, 3]
    inv = 1.0 / cos_rows[:, None, None]
    sn = sin_rows[:, None, None]
    cp = cos_pad[:, None, None]

    def middle(a):
        return a[1:-1, :, 1:-1]

    def east(a):
        return a[1:-1, :, 2:]

    def west(a):
        return a[1:-1, :, :-2]

    def north(a):
        return a[2:, :, 1:-1]

    def south(a):
        return a[:-2, :, 1:-1]

    flux_x = u * h
    flux_y = v * h * cp
    h_new = middle(h) - KX * inv * (east(flux_x) - west(flux_x)) - KY * inv * (north(flux_y) - south(flux_y))
    u_new = middle(u) - KX * inv * (east(h) - west(h)) + FC * sn * middle(v)
    v_new = middle(v) - KY * (north(h) - south(h)) - FC * sn * middle(u)
    q_new = middle(q) - KX * inv * middle(u) * (east(q) - west(q)) - KY * middle(v) * (north(q) - south(q))
    return jnp.stack([u_new, v_new, h_new, q_new], axis=1)


def damp_rows(fields, band_width, strength):
    taps = jnp.arange(-MAXB, MAXB + 1).astype(jnp.float32)
    weights = jnp.maximum(band_width[:, None] + 1.0 - jnp.abs(taps)[None, :], 0.0) / (band_width[:, None] + 1.0) ** 2
    padded = jnp.concatenate([fields[..., -MAXB:], fields, fields[..., :MAXB]], axis=3)

    def add_tap(tap, total):
        weight = lax.dynamic_index_in_dim(weights, tap, 1, keepdims=False)
        return total + weight[:, None, None, None] * lax.dynamic_slice_in_dim(padded, tap, NLON, 3)

    smooth = lax.fori_loop(0, 2 * MAXB + 1, add_tap, jnp.zeros_like(fields))
    return fields + strength[:, None, None, None] * (smooth - fields)


def reference(state, band, damping):
    wrapped = jnp.concatenate([state[..., -1:], state, state[..., :1]], axis=3)
    padded = jnp.pad(wrapped, ((1, 1), (0, 0), (0, 0), (0, 0)))
    rows = jnp.arange(-1, NLAT + 1).astype(jnp.float32)
    angle = math.pi * ((rows + 0.5) / NLAT - 0.5)
    cos_pad = jnp.cos(angle)
    stepped = advance_cells(padded, cos_pad[1:-1], jnp.sin(angle[1:-1]), cos_pad)
    quarter = NLAT // 4
    band_float = band.astype(jnp.float32)
    southern = damp_rows(stepped[:quarter], band_float[:quarter], damping[:quarter])
    northern = damp_rows(stepped[3 * quarter:], band_float[quarter:], damping[quarter:])
    return jnp.concatenate([southern, stepped[quarter:3 * quarter], northern], axis=0)
```

```python
import functools
import math

import jax
import jax.numpy as jnp
import numpy as np
from jax import lax
from jax.experimental import pallas as pl
from jax.experimental.pallas import tpu as pltpu
from jax.sharding import PartitionSpec as P

MAXB = 32
KX = 0.004
KY = 0.1
FC = 0.2

NLON_DEV = 8
NLAT_DEV = 16
ROWS = 32
NF = 4
LEV = 16
COLS = 360
LAST = COLS - 256
CHUNK = 4
NCHUNK = ROWS // CHUNK
MESH = pl.DeviceIdType.MESH
F32 = jnp.float32
BF16 = jnp.bfloat16


def row_table():
    total = ROWS * NLAT_DEV
    rows = np.arange(-1, total + 1, dtype=np.float32)
    angle = np.float32(math.pi) * ((rows + np.float32(0.5)) / np.float32(total) - np.float32(0.5))
    cos = np.cos(angle.astype(np.float64)).astype(np.float32)
    sin = np.sin(angle.astype(np.float64)).astype(np.float32)
    inv = np.float32(1.0) / cos
    table = np.zeros((NLAT_DEV, 8, 128), np.float32)
    for lat in range(NLAT_DEV):
        pad = slice(lat * ROWS, lat * ROWS + ROWS + 2)
        mid = slice(lat * ROWS + 1, lat * ROWS + ROWS + 1)
        table[lat, 0, : ROWS + 2] = cos[pad]
        table[lat, 1, :ROWS] = np.float32(KX) * inv[mid]
        table[lat, 2, :ROWS] = np.float32(KY) * inv[mid]
        table[lat, 3, :ROWS] = np.float32(FC) * sin[mid]
    return table


def kernel(
    state, band_hbm, damping_hbm, table_hbm, out,
    buf, to_east, to_west, from_west, from_east, x_east, x_west, xf_west, xf_east,
    edge, near, far, band, damping, table,
    load_sem, small_sem, send_sem, recv_sem, row_send, row_recv, x_send, x_recv, corner_send, corner_recv, ready,
):
    lon, lat = lax.axis_index("lon"), lax.axis_index("lat")
    east, west = lax.rem(lon + 1, NLON_DEV), lax.rem(lon + NLON_DEV - 1, NLON_DEV)
    north, south = lax.rem(lat + 1, NLAT_DEV), lax.rem(lat + NLAT_DEV - 1, NLAT_DEV)
    has_north, has_south = lat < NLAT_DEV - 1, lat > 0

    def at(a, b):
        return {"lon": a, "lat": b}

    def load(c):
        rows = pl.ds(c * CHUNK, CHUNK)
        return pltpu.make_async_copy(
            state.at[rows], buf.at[pl.ds(c * CHUNK + 1, CHUNK)], load_sem.at[c]
        )

    smalls = [
        pltpu.make_async_copy(band_hbm, band, small_sem.at[0]),
        pltpu.make_async_copy(damping_hbm, damping, small_sem.at[1]),
        pltpu.make_async_copy(table_hbm.at[lat], table, small_sem.at[2]),
    ]
    for c in range(NCHUNK):
        load(c).start()
    for copy in smalls:
        copy.start()

    barrier = pltpu.get_barrier_semaphore()
    for neighbour in (east, west):
        pl.semaphore_signal(barrier, 1, device_id=at(neighbour, lat), device_id_type=MESH)

    @pl.when(has_north)
    def _():
        pl.semaphore_signal(barrier, 1, device_id=at(lon, north), device_id_type=MESH)

    k = lax.broadcasted_iota(jnp.int32, (256, 128), 0)
    n = lax.broadcasted_iota(jnp.int32, (256, 128), 1)
    place = jnp.where(k < 192, k, k - 256)
    near[...] = jnp.minimum(jnp.abs(place - n), 255).astype(F32).astype(BF16)
    k = lax.broadcasted_iota(jnp.int32, (128, 256), 0)
    n = lax.broadcasted_iota(jnp.int32, (128, 256), 1)
    place = jnp.where(k >= 96, k - 128, jnp.where(k == 0, 0, jnp.where((k >= 31) & (k < 64), k + 328, 10000)))
    column = jnp.where(n < 128, n, n + 128)
    far[...] = jnp.minimum(jnp.abs(place - column), 255).astype(F32).astype(BF16)

    @pl.when(~has_south)
    def _():
        buf[0, 1:4] = jnp.zeros((3, LEV, COLS), F32)

    @pl.when(~has_north)
    def _():
        buf[ROWS + 1, 1:4] = jnp.zeros((3, LEV, COLS), F32)

    pl.semaphore_wait(barrier, 2 + jnp.where(has_south, 1, 0))

    def row_copy(i, target):
        source = state.at[ROWS - 1 if i == 0 else 0, pl.ds(1, 3)]
        goal = buf.at[0 if i == 0 else ROWS + 1, pl.ds(1, 3)]
        return pltpu.make_async_remote_copy(
            source, goal, row_send.at[i], row_recv.at[i], device_id=at(lon, target), device_id_type=MESH
        )

    @pl.when(has_south)
    def _():
        row_copy(1, south).start()
        pl.semaphore_signal(ready, 1, device_id=at(lon, south), device_id_type=MESH)

    lane = lax.broadcasted_iota(jnp.int32, (LEV, 128), 1)

    def tile(row, field, t):
        if t < 2:
            return buf[row, field, :, t * 128 : (t + 1) * 128]
        return jnp.concatenate([buf[row, field, :, 256:COLS], jnp.zeros((LEV, 128 - LAST), F32)], axis=1)

    def roll(a, shift):
        return pltpu.roll(a, shift, 1)

    def fixed(a, shift):
        return a if shift % 128 == 0 else pltpu.roll(a, shift % 128, 1)

    def pack(row, fields=range(NF)):
        for_east = jnp.zeros((LEV, 128), F32)
        for_west = jnp.zeros((LEV, 128), F32)
        for f in fields:
            here = (lane >= 32 * f) & (lane < 32 * f + 32)
            for_east = jnp.where(here, fixed(tile(row, f, 2), 32 * f - (LAST - 32)), for_east)
            for_west = jnp.where(here, fixed(tile(row, f, 0), 32 * f), for_west)
        return for_east, for_west

    def chunk_copy(c, i):
        source, goal, target = ((to_east, from_west, east), (to_west, from_east, west))[i]
        rows = pl.ds(c * CHUNK, CHUNK)
        return pltpu.make_async_remote_copy(
            source.at[rows], goal.at[rows], send_sem.at[i, c], recv_sem.at[i, c],
            device_id=at(target, lat), device_id_type=MESH,
        )

    def corner_copy(i, side):
        source, goal, target = ((to_east, from_west, east), (to_west, from_east, west))[side]
        return pltpu.make_async_remote_copy(
            source.at[ROWS + i], goal.at[ROWS + i], corner_send.at[side, i], corner_recv.at[side, i],
            device_id=at(target, lat), device_id_type=MESH,
        )

    def x_copy(side):
        source, goal, target = ((x_east, xf_west, east), (x_west, xf_east, west))[side]
        return pltpu.make_async_remote_copy(
            source, goal, x_send.at[side], x_recv.at[side], device_id=at(target, lat), device_id_type=MESH
        )

    def pack_chunk(c, carry):
        xe, xw = carry
        load(c).wait()
        for i in range(CHUNK):
            r = c * CHUNK + i
            to_east[r], to_west[r] = pack(r + 1)
            for slot, f in enumerate((0, 2, 3)):
                goal = 32 * slot + r
                here = lane == goal
                xe = jnp.where(here, roll(tile(r + 1, f, 2), lax.rem(goal + 256 - (LAST - 33), 128)), xe)
                xw = jnp.where(here, roll(tile(r + 1, f, 0), lax.rem(goal + 256 - 32, 128)), xw)
        chunk_copy(c, 0).start()
        chunk_copy(c, 1).start()
        return xe, xw

    xe, xw = lax.fori_loop(0, NCHUNK, pack_chunk, (jnp.zeros((LEV, 128), F32),) * 2)
    x_east[...] = xe
    x_west[...] = xw
    x_copy(0).start()
    x_copy(1).start()
    for copy in smalls:
        copy.wait()

    polar = (lat < NLAT_DEV // 4) | (lat >= NLAT_DEV - NLAT_DEV // 4)
    first = jnp.where(lat < NLAT_DEV // 4, lat * ROWS, jnp.where(polar, lat * ROWS - 256, 0))

    def coefficients(r):
        width = jnp.full((LEV, 128), band[first + r], jnp.int32).astype(F32) + 1.0
        strength = jnp.full((LEV, 128), jnp.where(polar, damping[first + r], 0.0), F32)
        return width, 1.0 - strength, strength / (width * width)

    def weights(distances, width):
        top = width.astype(BF16)
        rows, columns = distances.shape
        top = jnp.concatenate([top] * (rows // LEV), axis=0)
        top = jnp.concatenate([top] * (columns // 128), axis=1)
        return jnp.maximum(top - distances[...], jnp.zeros((), BF16))

    def step(r, mid, up, down, diff):
        kx, ky, fs = table[1, r], table[2, r], table[3, r]
        u, v, h, q = (mid(f) for f in range(NF))
        vn, hn, qn = (up(f) for f in (1, 2, 3))
        vs, hs, qs = (down(f) for f in (1, 2, 3))
        flux = vn * hn * table[0, r + 2] - vs * hs * table[0, r]
        d_flux, d_h, d_q = diff
        h_new = h - kx * d_flux - ky * flux
        u_new = u - kx * d_h + fs * v
        v_new = v - KY * (hn - hs) - fs * u
        q_new = q - kx * u * d_q - KY * v * (qn - qs)
        return u_new, v_new, h_new, q_new

    def halves(a):
        high = a.astype(BF16)
        return high, (a - high.astype(F32)).astype(BF16)

    def product(left, right):
        return jnp.dot(left, right, preferred_element_type=F32)

    def early(r):
        row = r + 1
        width, keep, gain = coefficients(r)
        mids = [[tile(row, f, t) for t in range(3)] for f in range(NF)]

        def difference(tiles):
            lo = [roll(a, 127) for a in tiles]
            hi = [roll(a, 1) for a in tiles]
            result = []
            for t in range(3):
                e = lo[t] if t == 2 else jnp.where(lane == 127, lo[t + 1], lo[t])
                w = hi[t] if t == 0 else jnp.where(lane == 0, hi[t - 1], hi[t])
                result.append(e - w)
            return result

        d_flux = difference([mids[0][t] * mids[2][t] for t in range(3)])
        d_h = difference(mids[2])
        d_q = difference(mids[3])
        stepped = []
        for t in range(3):
            values = step(
                r, lambda f: mids[f][t], lambda f: tile(row + 1, f, t), lambda f: tile(row - 1, f, t),
                (d_flux[t], d_h[t], d_q[t]),
            )
            if t == 0:
                values = [jnp.where(lane == 0, 0.0, a) for a in values]
            if t == 2:
                values = [jnp.where(lane >= LAST - 1, 0.0, a) for a in values]
            stepped.append(values)
        right = weights(near, width)
        parts = [[halves(a) for a in values] for values in stepped]
        zero = jnp.zeros((LEV, 128), BF16)

        def left(half):
            blocks = []
            for t in range(3):
                for f in range(NF):
                    after = parts[t + 1][f][half] if t < 2 else zero
                    before = parts[t - 1][f][half] if t > 0 else zero
                    side = jnp.where(lane < 64, after, before)
                    blocks.append(jnp.concatenate([parts[t][f][half], side], axis=1))
            return jnp.concatenate(blocks, axis=0)

        smooth = product(left(0), right) + product(left(1), right)
        for t in range(3):
            for f in range(NF):
                place = (t * NF + f) * LEV
                value = keep * stepped[t][f] + gain * smooth[place : place + LEV]
                if t < 2:
                    out[r, f, :, t * 128 : (t + 1) * 128] = value
                else:
                    out[r, f, :, 256:COLS] = value[:, :LAST]

    def unpack(slot, row, fields=range(NF), extra=None):
        got_west, got_east = from_west[slot], from_east[slot]
        for f in fields:
            own = jnp.where(lane < 2, tile(row, f, 0), fixed(tile(row, f, 2), 31 - (LAST - 1)))
            halo = jnp.where(lane >= 96, fixed(got_west, 96 - 32 * f), fixed(got_east, 32 - 32 * f))
            value = jnp.where(lane < 32, own, halo)
            if extra is not None and f != 1:
                goal = 32 * (0, None, 1, 2)[f] + extra
                value = jnp.where(lane == 95, roll(xf_west[...], lax.rem(95 + 256 - goal, 128)), value)
                value = jnp.where(lane == 64, roll(xf_east[...], lax.rem(64 + 256 - goal, 128)), value)
            edge[row, f] = value

    def late(r):
        row = r + 1
        width, keep, gain = coefficients(r)

        def difference(a):
            return roll(a, 127) - roll(a, 1)

        mids = [edge[row, f] for f in range(NF)]
        stepped = step(
            r, lambda f: mids[f], lambda f: edge[row + 1, f], lambda f: edge[row - 1, f],
            (difference(mids[0] * mids[2]), difference(mids[2]), difference(mids[3])),
        )
        right = weights(far, width)
        parts = [halves(a) for a in stepped]
        smooth = product(jnp.concatenate([p[0] for p in parts], axis=0), right) + product(
            jnp.concatenate([p[1] for p in parts], axis=0), right
        )
        for f in range(NF):
            more = gain * smooth[f * LEV : (f + 1) * LEV, :128] + jnp.where(lane == 0, keep * stepped[f], 0.0)
            out[r, f, :, 0:128] = out[r, f, :, 0:128] + more
            last = roll(stepped[f], LAST - 1 - 31)
            more = gain * smooth[f * LEV : (f + 1) * LEV, 128:] + jnp.where(lane == LAST - 1, keep * last, 0.0)
            out[r, f, :, 256:COLS] = out[r, f, :, 256:COLS] + more[:, :LAST]

    def rows(begin, end, body):
        def run(r, carry):
            body(r)
            return carry

        lax.fori_loop(begin, end, run, 0)

    rows(1, 8, early)

    @pl.when(has_north)
    def _():
        pl.semaphore_wait(ready, 1)
        row_copy(0, north).start()

    rows(8, 22, early)

    @pl.when(has_north)
    def _():
        row_copy(1, north).wait_recv()

    @pl.when(has_south)
    def _():
        row_copy(0, south).wait_recv()

    for i, row in enumerate((0, ROWS + 1)):
        to_east[ROWS + i], to_west[ROWS + i] = pack(row, (1, 2, 3))
        for side in range(2):
            corner_copy(i, side).start()
    rows(22, ROWS, early)
    early(0)

    for side in range(2):
        x_copy(side).wait()

    def late_chunk(c, carry):
        for side in range(2):
            chunk_copy(c, side).wait()
        for i in range(CHUNK):
            unpack(c * CHUNK + i, c * CHUNK + i + 1, extra=c * CHUNK + i)
        rows(jnp.maximum(c * CHUNK - 1, 1), c * CHUNK + CHUNK - 1, late)
        return carry

    lax.fori_loop(0, NCHUNK, late_chunk, 0)
    for i, row in enumerate((0, ROWS + 1)):
        for side in range(2):
            corner_copy(i, side).wait()
        unpack(ROWS + i, row, (1, 2, 3))
    late(0)
    late(ROWS - 1)

    @pl.when(has_north)
    def _():
        row_copy(0, north).wait_send()

    @pl.when(has_south)
    def _():
        row_copy(1, south).wait_send()


def shards(state, band, damping):
    hbm = pl.BlockSpec(memory_space=pl.ANY)
    packed = pltpu.VMEM((ROWS + 2, LEV, 128), F32)
    extra = pltpu.VMEM((LEV, 128), F32)
    dma = pltpu.SemaphoreType.DMA
    return pl.pallas_call(
        kernel,
        out_shape=pltpu.VMEM(state.shape, F32),
        in_specs=[hbm] * 4,
        out_specs=pl.BlockSpec(memory_space=pltpu.VMEM),
        scratch_shapes=[
            pltpu.VMEM((ROWS + 2, NF, LEV, COLS), F32),
            packed, packed, packed, packed,
            extra, extra, extra, extra,
            pltpu.VMEM((ROWS + 2, NF, LEV, 128), F32),
            pltpu.VMEM((256, 128), BF16),
            pltpu.VMEM((128, 256), BF16),
            pltpu.SMEM((256,), jnp.int32),
            pltpu.SMEM((256,), F32),
            pltpu.SMEM((8, 128), F32),
            dma((NCHUNK,)), dma((3,)),
            dma((2, NCHUNK)), dma((2, NCHUNK)),
            dma((2,)), dma((2,)),
            dma((2,)), dma((2,)),
            dma((2, 2)), dma((2, 2)),
            pltpu.SemaphoreType.REGULAR,
        ],
        compiler_params=pltpu.CompilerParams(
            collective_id=0, has_side_effects=True, vmem_limit_bytes=32 * 1024 * 1024
        ),
    )(state, band, damping, jnp.asarray(row_table()))


def solution(mesh):
    in_specs = (P("lat", None, None, "lon"), P(), P())
    out_specs = P("lat", None, None, "lon")
    return jax.shard_map(shards, mesh=mesh, in_specs=in_specs, out_specs=out_specs, check_vma=False)
```

```python
import functools
import math

import jax
import jax.numpy as jnp
import numpy as np
from jax import lax
from jax.experimental import pallas as pl
from jax.experimental.pallas import tpu as pltpu
from jax.sharding import PartitionSpec as P

MAXB = 32
KX = 0.004
KY = 0.1
FC = 0.2

NLON_DEV = 8
NLAT_DEV = 16
NX = 4
ROWS = 32
NF = 4
LEV = 16
COLS = 360
LAST = COLS - 256
CHUNK = 2
NCHUNK = ROWS // CHUNK
GROUP = 8
MESH = pl.DeviceIdType.MESH
F32 = jnp.float32
BF16 = jnp.bfloat16


def row_table():
    total = ROWS * NLAT_DEV
    rows = np.arange(-1, total + 1, dtype=np.float32)
    angle = np.float32(math.pi) * ((rows + np.float32(0.5)) / np.float32(total) - np.float32(0.5))
    cos = np.cos(angle.astype(np.float64)).astype(np.float32)
    sin = np.sin(angle.astype(np.float64)).astype(np.float32)
    inv = np.float32(1.0) / cos
    table = np.zeros((NLAT_DEV, 8, 128), np.float32)
    for lat in range(NLAT_DEV):
        pad = slice(lat * ROWS, lat * ROWS + ROWS + 2)
        mid = slice(lat * ROWS + 1, lat * ROWS + ROWS + 1)
        table[lat, 0, : ROWS + 2] = cos[pad]
        table[lat, 1, :ROWS] = np.float32(KX) * inv[mid]
        table[lat, 2, :ROWS] = np.float32(KY) * inv[mid]
        table[lat, 3, :ROWS] = np.float32(FC) * sin[mid]
    return table


def kernel(
    state, band_hbm, damping_hbm, table_hbm, out,
    buf, to_east, to_west, from_west, from_east, x_east, x_west, xf_west, xf_east, x_both,
    edge, near, far, band, damping, table,
    load_sem, small_sem, send_sem, recv_sem, row_send, row_recv, x_send, x_recv, corner_send, corner_recv, ready,
):
    lon, lat = lax.axis_index("lon"), lax.axis_index("lat")
    east, west = lax.rem(lon + 1, NLON_DEV), lax.rem(lon + NLON_DEV - 1, NLON_DEV)
    north, south = lax.rem(lat + 1, NLAT_DEV), lax.rem(lat + NLAT_DEV - 1, NLAT_DEV)
    has_north, has_south = lat < NLAT_DEV - 1, lat > 0
    x = lax.rem(lat, NX)
    first_north, first_south = x < NX - 1, (x == 0) & has_south
    second_north, second_south = (x == NX - 1) & has_north, x > 0

    def at(a, b):
        return {"lon": a, "lat": b}

    def load(c):
        rows = pl.ds(c * CHUNK, CHUNK)
        return pltpu.make_async_copy(
            state.at[rows], buf.at[pl.ds(c * CHUNK + 1, CHUNK)], load_sem.at[c]
        )

    smalls = [
        pltpu.make_async_copy(band_hbm, band, small_sem.at[0]),
        pltpu.make_async_copy(damping_hbm, damping, small_sem.at[1]),
        pltpu.make_async_copy(table_hbm.at[lat], table, small_sem.at[2]),
    ]
    for c in range(NCHUNK):
        load(c).start()
    for copy in smalls:
        copy.start()

    barrier = pltpu.get_barrier_semaphore()
    for neighbour in (east, west):
        pl.semaphore_signal(barrier, 1, device_id=at(neighbour, lat), device_id_type=MESH)

    @pl.when(first_north)
    def _():
        pl.semaphore_signal(barrier, 1, device_id=at(lon, north), device_id_type=MESH)

    @pl.when(first_south)
    def _():
        pl.semaphore_signal(barrier, 1, device_id=at(lon, south), device_id_type=MESH)

    k = lax.broadcasted_iota(jnp.int32, (256, 128), 0)
    n = lax.broadcasted_iota(jnp.int32, (256, 128), 1)
    place = jnp.where(k < 192, k, k - 256)
    near[...] = jnp.minimum(jnp.abs(place - n), 255).astype(F32).astype(BF16)
    k = lax.broadcasted_iota(jnp.int32, (128, 256), 0)
    n = lax.broadcasted_iota(jnp.int32, (128, 256), 1)
    place = jnp.where(k >= 96, k - 128, jnp.where(k == 0, 0, jnp.where((k >= 30) & (k < 63), k + 329, 10000)))
    column = jnp.where(n < 128, n, n + 128)
    far[...] = jnp.minimum(jnp.abs(place - column), 255).astype(F32).astype(BF16)

    @pl.when(~has_south)
    def _():
        buf[0, 1:4] = jnp.zeros((3, LEV, COLS), F32)

    @pl.when(~has_north)
    def _():
        buf[ROWS + 1, 1:4] = jnp.zeros((3, LEV, COLS), F32)

    pl.semaphore_wait(barrier, 2 + jnp.where(second_south, 1, 0) + jnp.where(second_north, 1, 0))

    def row_copy(i, target):
        source = state.at[ROWS - 1 if i == 0 else 0, pl.ds(1, 3)]
        goal = buf.at[0 if i == 0 else ROWS + 1, pl.ds(1, 3)]
        return pltpu.make_async_remote_copy(
            source, goal, row_send.at[i], row_recv.at[i], device_id=at(lon, target), device_id_type=MESH
        )

    @pl.when(second_south)
    def _():
        row_copy(1, south).start()
        pl.semaphore_signal(ready.at[0], 1, device_id=at(lon, south), device_id_type=MESH)

    @pl.when(second_north)
    def _():
        row_copy(0, north).start()
        pl.semaphore_signal(ready.at[1], 1, device_id=at(lon, north), device_id_type=MESH)

    lane = lax.broadcasted_iota(jnp.int32, (LEV, 128), 1)

    def tile(row, field, t):
        if t < 2:
            return buf[row, field, :, t * 128 : (t + 1) * 128]
        return jnp.concatenate([buf[row, field, :, 256:COLS], jnp.zeros((LEV, 128 - LAST), F32)], axis=1)

    def roll(a, shift):
        return pltpu.roll(a, shift, 1)

    def fixed(a, shift):
        return a if shift % 128 == 0 else pltpu.roll(a, shift % 128, 1)

    def pack(row, fields=range(NF)):
        for_east = jnp.zeros((LEV, 128), F32)
        for_west = jnp.zeros((LEV, 128), F32)
        for f in fields:
            here = (lane >= 32 * f) & (lane < 32 * f + 32)
            for_east = jnp.where(here, fixed(tile(row, f, 2), 32 * f - (LAST - 32)), for_east)
            for_west = jnp.where(here, fixed(tile(row, f, 0), 32 * f), for_west)
        return for_east, for_west

    def chunk_copy(c, i):
        source, goal, target = ((to_east, from_west, east), (to_west, from_east, west))[i]
        rows = pl.ds(c * CHUNK, CHUNK)
        return pltpu.make_async_remote_copy(
            source.at[rows], goal.at[rows], send_sem.at[i, c], recv_sem.at[i, c],
            device_id=at(target, lat), device_id_type=MESH,
        )

    def corner_copy(i, side):
        source, goal, target = ((to_east, from_west, east), (to_west, from_east, west))[side]
        return pltpu.make_async_remote_copy(
            source.at[ROWS + i], goal.at[ROWS + i], corner_send.at[side, i], corner_recv.at[side, i],
            device_id=at(target, lat), device_id_type=MESH,
        )

    def x_copy(side):
        source, goal, target = ((x_east, xf_west, east), (x_west, xf_east, west))[side]
        return pltpu.make_async_remote_copy(
            source, goal, x_send.at[side], x_recv.at[side], device_id=at(target, lat), device_id_type=MESH
        )

    def pack_chunk(c, carry):
        xe, xw = carry
        load(c).wait()
        for i in range(CHUNK):
            r = c * CHUNK + i
            to_east[r], to_west[r] = pack(r + 1)
            for slot, f in enumerate((0, 2, 3)):
                goal = 32 * slot + r
                here = lane == goal
                xe = jnp.where(here, roll(tile(r + 1, f, 2), lax.rem(goal + 256 - (LAST - 33), 128)), xe)
                xw = jnp.where(here, roll(tile(r + 1, f, 0), lax.rem(goal + 256 - 32, 128)), xw)
        chunk_copy(c, 0).start()
        chunk_copy(c, 1).start()
        return xe, xw

    xe, xw = lax.fori_loop(0, NCHUNK, pack_chunk, (jnp.zeros((LEV, 128), F32),) * 2)
    x_east[...] = xe
    x_west[...] = xw
    x_copy(0).start()
    x_copy(1).start()
    for copy in smalls:
        copy.wait()

    polar = (lat < NLAT_DEV // 4) | (lat >= NLAT_DEV - NLAT_DEV // 4)
    first = jnp.where(lat < NLAT_DEV // 4, lat * ROWS, jnp.where(polar, lat * ROWS - 256, 0))

    def coefficients(r):
        width = jnp.full((LEV, 128), band[first + r], jnp.int32).astype(F32) + 1.0
        strength = jnp.full((LEV, 128), jnp.where(polar, damping[first + r], 0.0), F32)
        return width, 1.0 - strength, strength / (width * width)

    def weights(distances, width):
        top = width.astype(BF16)
        rows, columns = distances.shape
        top = jnp.concatenate([top] * (rows // LEV), axis=0)
        top = jnp.concatenate([top] * (columns // 128), axis=1)
        return jnp.maximum(top - distances[...], jnp.zeros((), BF16))

    def step(r, mid, up, down, diff):
        kx, ky, fs = table[1, r], table[2, r], table[3, r]
        u, v, h, q = (mid(f) for f in range(NF))
        vn, hn, qn = (up(f) for f in (1, 2, 3))
        vs, hs, qs = (down(f) for f in (1, 2, 3))
        flux = vn * hn * table[0, r + 2] - vs * hs * table[0, r]
        d_flux, d_h, d_q = diff
        h_new = h - kx * d_flux - ky * flux
        u_new = u - kx * d_h + fs * v
        v_new = v - KY * (hn - hs) - fs * u
        q_new = q - kx * u * d_q - KY * v * (qn - qs)
        return u_new, v_new, h_new, q_new

    def halves(a):
        high = a.astype(BF16)
        return high, (a - high.astype(F32)).astype(BF16)

    def product(left, right):
        return jnp.dot(left, right, preferred_element_type=F32)

    def early(r):
        row = r + 1
        width, keep, gain = coefficients(r)
        mids = [[tile(row, f, t) for t in range(3)] for f in range(NF)]

        def difference(tiles):
            lo = [roll(a, 127) for a in tiles]
            hi = [roll(a, 1) for a in tiles]
            result = []
            for t in range(3):
                e = lo[t] if t == 2 else jnp.where(lane == 127, lo[t + 1], lo[t])
                w = hi[t] if t == 0 else jnp.where(lane == 0, hi[t - 1], hi[t])
                result.append(e - w)
            return result

        d_flux = difference([mids[0][t] * mids[2][t] for t in range(3)])
        d_h = difference(mids[2])
        d_q = difference(mids[3])
        stepped = []
        for t in range(3):
            values = step(
                r, lambda f: mids[f][t], lambda f: tile(row + 1, f, t), lambda f: tile(row - 1, f, t),
                (d_flux[t], d_h[t], d_q[t]),
            )
            if t == 0:
                values = [jnp.where(lane == 0, 0.0, a) for a in values]
            if t == 2:
                values = [jnp.where(lane >= LAST - 1, 0.0, a) for a in values]
            stepped.append(values)
        right = weights(near, width)
        parts = [[halves(a) for a in values] for values in stepped]
        zero = jnp.zeros((LEV, 128), BF16)

        def left(half):
            blocks = []
            for t in range(3):
                for f in range(NF):
                    after = parts[t + 1][f][half] if t < 2 else zero
                    before = parts[t - 1][f][half] if t > 0 else zero
                    side = jnp.where(lane < 64, after, before)
                    blocks.append(jnp.concatenate([parts[t][f][half], side], axis=1))
            return jnp.concatenate(blocks, axis=0)

        both = product(jnp.concatenate([left(0), left(1)], axis=0), right)
        smooth = both[: both.shape[0] // 2] + both[both.shape[0] // 2 :]
        for t in range(3):
            for f in range(NF):
                place = (t * NF + f) * LEV
                value = keep * stepped[t][f] + gain * smooth[place : place + LEV]
                if t < 2:
                    out[r, f, :, t * 128 : (t + 1) * 128] = value
                else:
                    out[r, f, :, 256:COLS] = value[:, :LAST]

    def unpack(slot, row, fields=range(NF), extra=None):
        got_west, got_east = from_west[slot], from_east[slot]
        for f in fields:
            own = jnp.where(lane < 2, tile(row, f, 0), fixed(tile(row, f, 2), 30 - (LAST - 1)))
            halo = jnp.where(lane >= 96, fixed(got_west, 96 - 32 * f), fixed(got_east, 31 - 32 * f))
            value = jnp.where(lane < 31, own, halo)
            if extra is not None and f != 1:
                outer = roll(x_both[(0, None, 1, 2)[f]], 63 - extra)
                value = jnp.where((lane == 63) | (lane == 95), outer, value)
            edge[row, f] = value

    def late(r):
        row = r + 1
        width, keep, gain = coefficients(r)

        def difference(a):
            return roll(a, 127) - roll(a, 1)

        mids = [edge[row, f] for f in range(NF)]
        stepped = step(
            r, lambda f: mids[f], lambda f: edge[row + 1, f], lambda f: edge[row - 1, f],
            (difference(mids[0] * mids[2]), difference(mids[2]), difference(mids[3])),
        )
        right = weights(far, width)
        parts = [halves(a) for a in stepped]
        left = jnp.concatenate([jnp.concatenate(p, axis=1) for p in parts], axis=0)
        smooth = product(left, jnp.concatenate([right, right], axis=0))
        for f in range(NF):
            more = gain * smooth[f * LEV : (f + 1) * LEV, :128] + jnp.where(lane == 0, keep * stepped[f], 0.0)
            out[r, f, :, 0:128] = out[r, f, :, 0:128] + more
            last = roll(stepped[f], LAST - 1 - 30)
            more = gain * smooth[f * LEV : (f + 1) * LEV, 128:] + jnp.where(lane == LAST - 1, keep * last, 0.0)
            out[r, f, :, 256:COLS] = out[r, f, :, 256:COLS] + more[:, :LAST]

    for i in range(GROUP):
        early(1 + i)

    @pl.when(first_north)
    def _():
        pl.semaphore_wait(ready.at[0], 1)
        row_copy(0, north).start()

    @pl.when(first_south)
    def _():
        pl.semaphore_wait(ready.at[1], 1)
        row_copy(1, south).start()

    def early_group(g, carry):
        for i in range(GROUP):
            early(g * GROUP + 1 + i)
        return carry

    lax.fori_loop(1, 3, early_group, 0)

    @pl.when(has_north)
    def _():
        row_copy(1, north).wait_recv()

    @pl.when(has_south)
    def _():
        row_copy(0, south).wait_recv()

    for i, row in enumerate((0, ROWS + 1)):
        to_east[ROWS + i], to_west[ROWS + i] = pack(row, (1, 2, 3))
        for side in range(2):
            corner_copy(i, side).start()
    for r in (*range(3 * GROUP + 1, ROWS), 0):
        early(r)

    for side in range(2):
        x_copy(side).wait()
    for slot in range(3):
        x_both[slot] = jnp.where(lane < 32, fixed(xf_east[...], -32 * slot), fixed(xf_west[...], 32 - 32 * slot))

    def arrived(c):
        for side in range(2):
            chunk_copy(c, side).wait()
        for i in range(CHUNK):
            unpack(c * CHUNK + i, c * CHUNK + i + 1, extra=c * CHUNK + i)

    arrived(0)

    def late_group(g, carry):
        for i in range(GROUP // CHUNK):
            for side in range(2):
                chunk_copy(g * (GROUP // CHUNK) + 1 + i, side).wait()
        for i in range(GROUP):
            r = g * GROUP + CHUNK + i
            unpack(r, r + 1, extra=r)
        for i in range(GROUP):
            late(g * GROUP + 1 + i)
        return carry

    lax.fori_loop(0, 3, late_group, 0)
    for c in range(3 * GROUP // CHUNK + 1, NCHUNK):
        arrived(c)
    for i, row in enumerate((0, ROWS + 1)):
        for side in range(2):
            corner_copy(i, side).wait()
        unpack(ROWS + i, row, (1, 2, 3))
    for r in (*range(3 * GROUP + 1, ROWS), 0):
        late(r)

    @pl.when(has_north)
    def _():
        row_copy(0, north).wait_send()

    @pl.when(has_south)
    def _():
        row_copy(1, south).wait_send()


def shards(state, band, damping):
    hbm = pl.BlockSpec(memory_space=pltpu.HBM)
    packed = pltpu.VMEM((ROWS + 2, LEV, 128), F32)
    extra = pltpu.VMEM((LEV, 128), F32)
    dma = pltpu.SemaphoreType.DMA
    return pl.pallas_call(
        kernel,
        out_shape=pltpu.VMEM(state.shape, F32),
        in_specs=[hbm] * 4,
        out_specs=pl.BlockSpec(memory_space=pltpu.VMEM),
        scratch_shapes=[
            pltpu.VMEM((ROWS + 2, NF, LEV, COLS), F32),
            packed, packed, packed, packed,
            extra, extra, extra, extra,
            pltpu.VMEM((3, LEV, 128), F32),
            pltpu.VMEM((ROWS + 2, NF, LEV, 128), F32),
            pltpu.VMEM((256, 128), BF16),
            pltpu.VMEM((128, 256), BF16),
            pltpu.SMEM((256,), jnp.int32),
            pltpu.SMEM((256,), F32),
            pltpu.SMEM((8, 128), F32),
            dma((NCHUNK,)), dma((3,)),
            dma((2, NCHUNK)), dma((2, NCHUNK)),
            dma((2,)), dma((2,)),
            dma((2,)), dma((2,)),
            dma((2, 2)), dma((2, 2)),
            pltpu.SemaphoreType.REGULAR((2,)),
        ],
        compiler_params=pltpu.CompilerParams(
            collective_id=0, has_side_effects=True, vmem_limit_bytes=60 * 1024 * 1024
        ),
    )(state, band, damping, jnp.asarray(row_table()))


def solution(mesh):
    in_specs = (P("lat", None, None, "lon"), P(), P())
    out_specs = P("lat", None, None, "lon")
    return jax.shard_map(shards, mesh=mesh, in_specs=in_specs, out_specs=out_specs, check_vma=False)
```

```python
import functools
import math

import jax
import jax.numpy as jnp
import numpy as np
from jax import lax
from jax.experimental import pallas as pl
from jax.experimental.pallas import tpu as pltpu
from jax.sharding import PartitionSpec as P

MAXB = 32
KX = 0.004
KY = 0.1
FC = 0.2

NLON_DEV = 8
NLAT_DEV = 16
NX = 4
ROWS = 32
NF = 4
LEV = 16
COLS = 360
LAST = COLS - 256
CHUNK = 4
NCHUNK = ROWS // CHUNK
GROUP = 8
MESH = pl.DeviceIdType.MESH
F32 = jnp.float32
BF16 = jnp.bfloat16


def row_table():
    total = ROWS * NLAT_DEV
    rows = np.arange(-1, total + 1, dtype=np.float32)
    angle = np.float32(math.pi) * ((rows + np.float32(0.5)) / np.float32(total) - np.float32(0.5))
    cos = np.cos(angle.astype(np.float64)).astype(np.float32)
    sin = np.sin(angle.astype(np.float64)).astype(np.float32)
    inv = np.float32(1.0) / cos
    table = np.zeros((NLAT_DEV, 8, 128), np.float32)
    for lat in range(NLAT_DEV):
        pad = slice(lat * ROWS, lat * ROWS + ROWS + 2)
        mid = slice(lat * ROWS + 1, lat * ROWS + ROWS + 1)
        table[lat, 0, : ROWS + 2] = cos[pad]
        table[lat, 1, :ROWS] = np.float32(KX) * inv[mid]
        table[lat, 2, :ROWS] = np.float32(KY) * inv[mid]
        table[lat, 3, :ROWS] = np.float32(FC) * sin[mid]
    return table


def kernel(
    state, band_hbm, damping_hbm, table_hbm, out,
    buf, to_east, to_west, from_west, from_east, x_east, x_west, xf_west, xf_east, x_both,
    edge, near, far, band, damping, table,
    load_sem, small_sem, send_sem, recv_sem, row_send, row_recv, x_send, x_recv, ready,
):
    lon, lat = lax.axis_index("lon"), lax.axis_index("lat")
    east, west = lax.rem(lon + 1, NLON_DEV), lax.rem(lon + NLON_DEV - 1, NLON_DEV)
    north, south = lax.rem(lat + 1, NLAT_DEV), lax.rem(lat + NLAT_DEV - 1, NLAT_DEV)
    has_north, has_south = lat < NLAT_DEV - 1, lat > 0
    x = lax.rem(lat, NX)
    polar = (lat < NLAT_DEV // 4) | (lat >= NLAT_DEV - NLAT_DEV // 4)
    crossing = ((x == NX - 1) & has_north) | ((x == 0) & has_south)
    last_south, first_mid = lat == NLAT_DEV // 4 - 1, lat == NLAT_DEV // 4
    first = ((x < NX - 1) | last_south, (x == 0) & has_south & ~first_mid, lon < NLON_DEV - 1, lon == 0)
    second = ((x == NX - 1) & has_north & ~last_south, (x > 0) | first_mid, lon == NLON_DEV - 1, lon > 0)
    others = ((lon, north), (lon, south), (east, lat), (west, lat))
    NORTH, SOUTH, EAST, WEST = range(4)
    OPPOSITE = (SOUTH, NORTH, WEST, EAST)

    def at(a, b):
        return {"lon": a, "lat": b}

    def load(c):
        rows = pl.ds(c * CHUNK, CHUNK)
        return pltpu.make_async_copy(
            state.at[rows], buf.at[pl.ds(c * CHUNK + 1, CHUNK)], load_sem.at[c]
        )

    smalls = [
        pltpu.make_async_copy(band_hbm, band, small_sem.at[0]),
        pltpu.make_async_copy(damping_hbm, damping, small_sem.at[1]),
        pltpu.make_async_copy(table_hbm.at[lat], table, small_sem.at[2]),
    ]
    for c in range(NCHUNK):
        load(c).start()
    for copy in smalls:
        copy.start()

    barrier = pltpu.get_barrier_semaphore()
    for side in range(4):

        @pl.when(first[side])
        def _():
            pl.semaphore_signal(barrier, 1, device_id=at(*others[side]), device_id_type=MESH)

    @pl.when(lon == 1)
    def _():
        pl.semaphore_signal(barrier, 1, device_id=at(west, lat), device_id_type=MESH)

    k = lax.broadcasted_iota(jnp.int32, (256, 128), 0)
    n = lax.broadcasted_iota(jnp.int32, (256, 128), 1)
    place = jnp.where(k < 192, k, k - 256)
    near[...] = jnp.minimum(jnp.abs(place - n), 255).astype(F32).astype(BF16)
    k = lax.broadcasted_iota(jnp.int32, (128, 256), 0)
    n = lax.broadcasted_iota(jnp.int32, (128, 256), 1)
    place = jnp.where(k >= 96, k - 128, jnp.where(k == 0, 0, jnp.where((k >= 30) & (k < 63), k + 329, 10000)))
    column = jnp.where(n < 128, n, n + 128)
    far[...] = jnp.minimum(jnp.abs(place - column), 255).astype(F32).astype(BF16)

    @pl.when(~has_south)
    def _():
        buf[0, 1:4] = jnp.zeros((3, LEV, COLS), F32)

    @pl.when(~has_north)
    def _():
        buf[ROWS + 1, 1:4] = jnp.zeros((3, LEV, COLS), F32)

    @pl.when(~polar)
    def _():
        from_west[...] = jnp.zeros(from_west.shape, F32)
        from_east[...] = jnp.zeros(from_east.shape, F32)

    pl.semaphore_wait(barrier, sum(jnp.where(flag, 1, 0) for flag in (*second, lon == 0)))

    def row_copy(i, target):
        source = state.at[ROWS - 1 if i == 0 else 0, pl.ds(1, 3)]
        goal = buf.at[0 if i == 0 else ROWS + 1, pl.ds(1, 3)]
        return pltpu.make_async_remote_copy(
            source, goal, row_send.at[i], row_recv.at[i], device_id=at(lon, target), device_id_type=MESH
        )

    @pl.when(second[SOUTH])
    def _():
        row_copy(1, south).start()

    @pl.when(second[NORTH])
    def _():
        row_copy(0, north).start()

    for side in range(4):

        @pl.when(second[side])
        def _():
            pl.semaphore_signal(ready.at[OPPOSITE[side]], 1, device_id=at(*others[side]), device_id_type=MESH)

    lane = lax.broadcasted_iota(jnp.int32, (LEV, 128), 1)

    def tile(row, field, t):
        if t < 2:
            return buf[row, field, :, t * 128 : (t + 1) * 128]
        return jnp.concatenate([buf[row, field, :, 256:COLS], jnp.zeros((LEV, 128 - LAST), F32)], axis=1)

    def roll(a, shift):
        return pltpu.roll(a, shift, 1)

    def fixed(a, shift):
        return a if shift % 128 == 0 else pltpu.roll(a, shift % 128, 1)

    def pack(row, fields=range(NF)):
        for_east = jnp.zeros((LEV, 128), F32)
        for_west = jnp.zeros((LEV, 128), F32)
        for f in fields:
            here = (lane >= 32 * f) & (lane < 32 * f + 32)
            for_east = jnp.where(here, fixed(tile(row, f, 2), 32 * f - (LAST - 32)), for_east)
            for_west = jnp.where(here, fixed(tile(row, f, 0), 32 * f), for_west)
        return for_east, for_west

    def chunk_copy(c, i):
        source, goal, target = ((to_east, from_west, east), (to_west, from_east, west))[i]
        rows = pl.ds(c * CHUNK, CHUNK)
        return pltpu.make_async_remote_copy(
            source.at[rows], goal.at[rows], send_sem.at[i, c], recv_sem.at[i, c],
            device_id=at(target, lat), device_id_type=MESH,
        )

    def corner_copy(i):
        source, goal, target = ((to_east, from_west, east), (to_west, from_east, west))[i]
        rows = pl.ds(ROWS, 2)
        return pltpu.make_async_remote_copy(
            source.at[rows], goal.at[rows], send_sem.at[i, NCHUNK], recv_sem.at[i, NCHUNK],
            device_id=at(target, lat), device_id_type=MESH,
        )

    def x_copy(side):
        source, goal, target = ((x_east, xf_west, east), (x_west, xf_east, west))[side]
        return pltpu.make_async_remote_copy(
            source, goal, x_send.at[side], x_recv.at[side], device_id=at(target, lat), device_id_type=MESH
        )

    def pack_chunk(c, carry):
        xe, xw = carry
        load(c).wait()
        for i in range(CHUNK):
            r = c * CHUNK + i
            to_east[r], to_west[r] = pack(r + 1)
            for slot, f in enumerate((0, 2, 3)):
                goal = 32 * slot + r
                here = lane == goal
                xe = jnp.where(here, roll(tile(r + 1, f, 2), lax.rem(goal + 256 - jnp.where(polar, LAST - 33, LAST - 1), 128)), xe)
                xw = jnp.where(here, roll(tile(r + 1, f, 0), lax.rem(goal + 256 - jnp.where(polar, 32, 0), 128)), xw)

        @pl.when(polar & second[EAST])
        def _():
            chunk_copy(c, 0).start()

        @pl.when(polar & second[WEST])
        def _():
            chunk_copy(c, 1).start()

        return xe, xw

    xe, xw = lax.fori_loop(0, NCHUNK, pack_chunk, (jnp.zeros((LEV, 128), F32),) * 2)
    x_east[...] = xe
    x_west[...] = xw

    def send_side(i):
        pl.semaphore_wait(ready.at[(EAST, WEST)[i]], 1)

        def send(c, carry):
            chunk_copy(c, i).start()
            return carry

        lax.fori_loop(0, jnp.where(polar, NCHUNK, 0), send, 0)
        x_copy(i).start()

    @pl.when(second[EAST])
    def _():
        x_copy(0).start()

    @pl.when(second[WEST])
    def _():
        x_copy(1).start()

    @pl.when(first[EAST])
    def _():
        send_side(0)

    @pl.when(first[NORTH] & ~last_south)
    def _():
        pl.semaphore_wait(ready.at[NORTH], 1)
        row_copy(0, north).start()

    @pl.when(first[WEST])
    def _():
        send_side(1)

    for copy in smalls:
        copy.wait()

    origin = jnp.where(lat < NLAT_DEV // 4, lat * ROWS, jnp.where(polar, lat * ROWS - 256, 0))

    def coefficients(r):
        width = jnp.full((LEV, 128), band[origin + r], jnp.int32).astype(F32) + 1.0
        strength = jnp.full((LEV, 128), jnp.where(polar, damping[origin + r], 0.0), F32)
        return width, 1.0 - strength, strength / (width * width)

    def weights(distances, width):
        top = width.astype(BF16)
        rows, columns = distances.shape
        top = jnp.concatenate([top] * (rows // LEV), axis=0)
        top = jnp.concatenate([top] * (columns // 128), axis=1)
        return jnp.maximum(top - distances[...], jnp.zeros((), BF16))

    def step(r, mid, up, down, diff):
        kx, ky, fs = table[1, r], table[2, r], table[3, r]
        u, v, h, q = (mid(f) for f in range(NF))
        vn, hn, qn = (up(f) for f in (1, 2, 3))
        vs, hs, qs = (down(f) for f in (1, 2, 3))
        flux = vn * hn * table[0, r + 2] - vs * hs * table[0, r]
        d_flux, d_h, d_q = diff
        h_new = h - kx * d_flux - ky * flux
        u_new = u - kx * d_h + fs * v
        v_new = v - KY * (hn - hs) - fs * u
        q_new = q - kx * u * d_q - KY * v * (qn - qs)
        return u_new, v_new, h_new, q_new

    def halves(a):
        high = a.astype(BF16)
        return high, (a - high.astype(F32)).astype(BF16)

    def product(left, right):
        return jnp.dot(left, right, preferred_element_type=F32)

    def early(r):
        row = r + 1
        width, keep, gain = coefficients(r)
        mids = [[tile(row, f, t) for t in range(3)] for f in range(NF)]

        def difference(tiles):
            lo = [roll(a, 127) for a in tiles]
            hi = [roll(a, 1) for a in tiles]
            result = []
            for t in range(3):
                e = lo[t] if t == 2 else jnp.where(lane == 127, lo[t + 1], lo[t])
                w = hi[t] if t == 0 else jnp.where(lane == 0, hi[t - 1], hi[t])
                result.append(e - w)
            return result

        d_flux = difference([mids[0][t] * mids[2][t] for t in range(3)])
        d_h = difference(mids[2])
        d_q = difference(mids[3])
        stepped = []
        for t in range(3):
            values = step(
                r, lambda f: mids[f][t], lambda f: tile(row + 1, f, t), lambda f: tile(row - 1, f, t),
                (d_flux[t], d_h[t], d_q[t]),
            )
            if t == 0:
                values = [jnp.where(lane == 0, 0.0, a) for a in values]
            if t == 2:
                values = [jnp.where(lane >= LAST - 1, 0.0, a) for a in values]
            stepped.append(values)
        right = weights(near, width)
        parts = [[halves(a) for a in values] for values in stepped]
        zero = jnp.zeros((LEV, 128), BF16)

        def left(half):
            blocks = []
            for t in range(3):
                for f in range(NF):
                    after = parts[t + 1][f][half] if t < 2 else zero
                    before = parts[t - 1][f][half] if t > 0 else zero
                    side = jnp.where(lane < 64, after, before)
                    blocks.append(jnp.concatenate([parts[t][f][half], side], axis=1))
            return jnp.concatenate(blocks, axis=0)

        both = product(jnp.concatenate([left(0), left(1)], axis=0), right)
        smooth = both[: both.shape[0] // 2] + both[both.shape[0] // 2 :]
        for t in range(3):
            for f in range(NF):
                place = (t * NF + f) * LEV
                value = keep * stepped[t][f] + gain * smooth[place : place + LEV]
                if t < 2:
                    out[r, f, :, t * 128 : (t + 1) * 128] = value
                else:
                    out[r, f, :, 256:COLS] = value[:, :LAST]

    outer_lanes = (lane == jnp.where(polar, 63, 31)) | (lane == jnp.where(polar, 95, 127))

    def unpack(slot):
        row = lax.rem(slot + 1, ROWS + 2)
        got_west, got_east = from_west[slot], from_east[slot]
        for f in range(NF):
            own = jnp.where(lane < 2, tile(row, f, 0), fixed(tile(row, f, 2), 30 - (LAST - 1)))
            halo = jnp.where(lane >= 96, fixed(got_west, 96 - 32 * f), fixed(got_east, 31 - 32 * f))
            value = jnp.where(lane < 31, own, halo)
            if f != 1:
                outer = roll(x_both[(0, None, 1, 2)[f]], jnp.where(polar, 63, 127) - slot)
                value = jnp.where(outer_lanes, outer, value)
            edge[row, f] = value

    def late(r):
        row = r + 1
        width, keep, gain = coefficients(r)

        def difference(a):
            return roll(a, 127) - roll(a, 1)

        mids = [edge[row, f] for f in range(NF)]
        stepped = step(
            r, lambda f: mids[f], lambda f: edge[row + 1, f], lambda f: edge[row - 1, f],
            (difference(mids[0] * mids[2]), difference(mids[2]), difference(mids[3])),
        )
        right = weights(far, width)
        parts = [halves(a) for a in stepped]
        left = jnp.concatenate([jnp.concatenate(p, axis=1) for p in parts], axis=0)
        smooth = product(left, jnp.concatenate([right, right], axis=0))
        for f in range(NF):
            more = gain * smooth[f * LEV : (f + 1) * LEV, :128] + jnp.where(lane == 0, keep * stepped[f], 0.0)
            out[r, f, :, 0:128] = out[r, f, :, 0:128] + more
            last = roll(stepped[f], LAST - 1 - 30)
            more = gain * smooth[f * LEV : (f + 1) * LEV, 128:] + jnp.where(lane == LAST - 1, keep * last, 0.0)
            out[r, f, :, 256:COLS] = out[r, f, :, 256:COLS] + more[:, :LAST]

    def early_group(g, carry):
        for i in range(GROUP):
            early(lax.rem(g * GROUP + 1 + i, ROWS))
        return carry

    def late_group(g, carry):
        for side in range(2):

            @pl.when(polar)
            def _():
                chunk_copy(2 * g + 1, side).wait()

            @pl.when(polar & (g < ROWS // GROUP - 1))
            def _():
                chunk_copy(2 * g + 2, side).wait()

            @pl.when(polar & (g == ROWS // GROUP - 1))
            def _():
                corner_copy(side).wait()

        for i in range(GROUP):
            unpack(g * GROUP + 2 + i)
            late(lax.rem(g * GROUP + 1 + i, ROWS))
        return carry

    lax.fori_loop(0, 1, early_group, 0)

    def outer_rows():
        @pl.when(has_north)
        def _():
            row_copy(1, north).wait_recv()

        @pl.when(has_south)
        def _():
            row_copy(0, south).wait_recv()

        @pl.when(polar)
        def _():
            for i, row in enumerate((ROWS + 1, 0)):
                to_east[ROWS + i], to_west[ROWS + i] = pack(row, (1, 2, 3))
            for side in range(2):
                corner_copy(side).start()

    lax.fori_loop(1, 2, early_group, 0)
    pl.when(~crossing)(outer_rows)
    lax.fori_loop(2, jnp.where(crossing, 3, 4), early_group, 0)

    @pl.when(last_south)
    def _():
        pl.semaphore_wait(ready.at[NORTH], 1)
        row_copy(0, north).start()

    @pl.when(first[SOUTH])
    def _():
        pl.semaphore_wait(ready.at[SOUTH], 1)
        row_copy(1, south).start()


    pl.when(crossing & polar)(outer_rows)

    for side in range(2):
        x_copy(side).wait()
    near_x = jnp.where(polar, xf_east[...], xf_west[...])
    far_x = jnp.where(polar, xf_west[...], xf_east[...])
    for slot in range(3):
        x_both[slot] = jnp.where(lane < 32, fixed(near_x, -32 * slot), fixed(far_x, 32 - 32 * slot))

    @pl.when(polar)
    def _():
        for side in range(2):
            chunk_copy(0, side).wait()

    for slot in range(2):
        unpack(slot)
    lax.fori_loop(0, 1, late_group, 0)
    lax.fori_loop(1, 3, late_group, 0)
    pl.when(crossing & ~polar)(outer_rows)
    lax.fori_loop(jnp.where(crossing, 3, 4), 4, early_group, 0)
    lax.fori_loop(3, 4, late_group, 0)

    @pl.when(has_north)
    def _():
        row_copy(0, north).wait_send()

    @pl.when(has_south)
    def _():
        row_copy(1, south).wait_send()


def shards(state, band, damping):
    hbm = pl.BlockSpec(memory_space=pltpu.HBM)
    packed = pltpu.VMEM((ROWS + 2, LEV, 128), F32)
    extra = pltpu.VMEM((LEV, 128), F32)
    dma = pltpu.SemaphoreType.DMA
    return pl.pallas_call(
        kernel,
        out_shape=pltpu.VMEM(state.shape, F32),
        in_specs=[hbm] * 4,
        out_specs=pl.BlockSpec(memory_space=pltpu.VMEM),
        scratch_shapes=[
            pltpu.VMEM((ROWS + 2, NF, LEV, COLS), F32),
            packed, packed, packed, packed,
            extra, extra, extra, extra,
            pltpu.VMEM((3, LEV, 128), F32),
            pltpu.VMEM((ROWS + 2, NF, LEV, 128), F32),
            pltpu.VMEM((256, 128), BF16),
            pltpu.VMEM((128, 256), BF16),
            pltpu.SMEM((256,), jnp.int32),
            pltpu.SMEM((256,), F32),
            pltpu.SMEM((8, 128), F32),
            dma((NCHUNK,)), dma((3,)),
            dma((2, NCHUNK + 1)), dma((2, NCHUNK + 1)),
            dma((2,)), dma((2,)),
            dma((2,)), dma((2,)),
            pltpu.SemaphoreType.REGULAR((4,)),
        ],
        compiler_params=pltpu.CompilerParams(
            collective_id=0, has_side_effects=True, vmem_limit_bytes=60 * 1024 * 1024
        ),
    )(state, band, damping, jnp.asarray(row_table()))


def solution(mesh):
    in_specs = (P("lat", None, None, "lon"), P(), P())
    out_specs = P("lat", None, None, "lon")
    return jax.shard_map(shards, mesh=mesh, in_specs=in_specs, out_specs=out_specs, check_vma=False)
```

```python
import functools
import math

import jax
import jax.numpy as jnp
import numpy as np
from jax import lax
from jax.experimental import pallas as pl
from jax.experimental.pallas import tpu as pltpu
from jax.sharding import PartitionSpec as P

MAXB = 32
KX = 0.004
KY = 0.1
FC = 0.2

NLON_DEV = 8
NLAT_DEV = 16
NX = 4
ROWS = 32
NF = 4
LEV = 16
COLS = 360
LAST = COLS - 256
CHUNK = 4
NCHUNK = ROWS // CHUNK
STAGES = (3, 5, 7, 8)
GROUP = 8
MESH = pl.DeviceIdType.MESH
F32 = jnp.float32
BF16 = jnp.bfloat16


def row_table():
    total = ROWS * NLAT_DEV
    rows = np.arange(-1, total + 1, dtype=np.float32)
    angle = np.float32(math.pi) * ((rows + np.float32(0.5)) / np.float32(total) - np.float32(0.5))
    cos = np.cos(angle.astype(np.float64)).astype(np.float32)
    sin = np.sin(angle.astype(np.float64)).astype(np.float32)
    inv = np.float32(1.0) / cos
    table = np.zeros((NLAT_DEV, 8, 128), np.float32)
    for lat in range(NLAT_DEV):
        pad = slice(lat * ROWS, lat * ROWS + ROWS + 2)
        mid = slice(lat * ROWS + 1, lat * ROWS + ROWS + 1)
        table[lat, 0, : ROWS + 2] = cos[pad]
        table[lat, 1, :ROWS] = np.float32(KX) * inv[mid]
        table[lat, 2, :ROWS] = np.float32(KY) * inv[mid]
        table[lat, 3, :ROWS] = np.float32(FC) * sin[mid]
    return table


def kernel(
    state, band_hbm, damping_hbm, table_hbm, out,
    buf, to_east, to_west, from_west, from_east, x_east, x_west, xf_west, xf_east, x_both,
    edge, near, far, band, damping, table,
    load_sem, small_sem, send_sem, recv_sem, row_send, row_recv, x_send, x_recv, ready,
):
    lon, lat = lax.axis_index("lon"), lax.axis_index("lat")
    east, west = lax.rem(lon + 1, NLON_DEV), lax.rem(lon + NLON_DEV - 1, NLON_DEV)
    north, south = lax.rem(lat + 1, NLAT_DEV), lax.rem(lat + NLAT_DEV - 1, NLAT_DEV)
    has_north, has_south = lat < NLAT_DEV - 1, lat > 0
    x = lax.rem(lat, NX)
    polar = (lat < NLAT_DEV // 4) | (lat >= NLAT_DEV - NLAT_DEV // 4)
    crossing = ((x == NX - 1) & has_north) | ((x == 0) & has_south)
    last_south, first_mid = lat == NLAT_DEV // 4 - 1, lat == NLAT_DEV // 4
    first = ((x < NX - 1) | last_south, (x == 0) & has_south & ~first_mid, lon < NLON_DEV - 1, lon == 0)
    second = ((x == NX - 1) & has_north & ~last_south, (x > 0) | first_mid, lon == NLON_DEV - 1, lon > 0)
    others = ((lon, north), (lon, south), (east, lat), (west, lat))
    NORTH, SOUTH, EAST, WEST = range(4)
    OPPOSITE = (SOUTH, NORTH, WEST, EAST)

    def at(a, b):
        return {"lon": a, "lat": b}

    def load(c):
        rows = pl.ds(c * CHUNK, CHUNK)
        return pltpu.make_async_copy(
            state.at[rows], buf.at[pl.ds(c * CHUNK + 1, CHUNK)], load_sem.at[c]
        )

    smalls = [
        pltpu.make_async_copy(band_hbm, band, small_sem.at[0]),
        pltpu.make_async_copy(damping_hbm, damping, small_sem.at[1]),
        pltpu.make_async_copy(table_hbm.at[lat], table, small_sem.at[2]),
    ]
    for c in range(NCHUNK):
        load(c).start()
    for copy in smalls:
        copy.start()

    barrier = pltpu.get_barrier_semaphore()
    for side in range(4):

        @pl.when(first[side])
        def _():
            pl.semaphore_signal(barrier, 1, device_id=at(*others[side]), device_id_type=MESH)

    @pl.when(lon == 1)
    def _():
        pl.semaphore_signal(barrier, 1, device_id=at(west, lat), device_id_type=MESH)

    k = lax.broadcasted_iota(jnp.int32, (256, 128), 0)
    n = lax.broadcasted_iota(jnp.int32, (256, 128), 1)
    place = jnp.where(k < 192, k, k - 256)
    near[...] = jnp.minimum(jnp.abs(place - n), 255).astype(F32).astype(BF16)
    k = lax.broadcasted_iota(jnp.int32, (128, 256), 0)
    n = lax.broadcasted_iota(jnp.int32, (128, 256), 1)
    place = jnp.where(k >= 96, k - 128, jnp.where(k == 0, 0, jnp.where((k >= 30) & (k < 63), k + 329, 10000)))
    column = jnp.where(n < 128, n, n + 128)
    far[...] = jnp.minimum(jnp.abs(place - column), 255).astype(F32).astype(BF16)

    @pl.when(~has_south)
    def _():
        buf[0, 1:4] = jnp.zeros((3, LEV, COLS), F32)

    @pl.when(~has_north)
    def _():
        buf[ROWS + 1, 1:4] = jnp.zeros((3, LEV, COLS), F32)

    @pl.when(~polar)
    def _():
        from_west[...] = jnp.zeros(from_west.shape, F32)
        from_east[...] = jnp.zeros(from_east.shape, F32)

    pl.semaphore_wait(barrier, sum(jnp.where(flag, 1, 0) for flag in (*second, lon == 0)))

    def row_copy(i, target):
        source = state.at[ROWS - 1 if i == 0 else 0, pl.ds(1, 3)]
        goal = buf.at[0 if i == 0 else ROWS + 1, pl.ds(1, 3)]
        return pltpu.make_async_remote_copy(
            source, goal, row_send.at[i], row_recv.at[i], device_id=at(lon, target), device_id_type=MESH
        )

    @pl.when(second[SOUTH])
    def _():
        row_copy(1, south).start()

    @pl.when(second[NORTH])
    def _():
        row_copy(0, north).start()

    for side in range(4):

        @pl.when(second[side])
        def _():
            pl.semaphore_signal(ready.at[OPPOSITE[side]], 1, device_id=at(*others[side]), device_id_type=MESH)

    lane = lax.broadcasted_iota(jnp.int32, (LEV, 128), 1)

    def tile(row, field, t):
        if t < 2:
            return buf[row, field, :, t * 128 : (t + 1) * 128]
        return jnp.concatenate([buf[row, field, :, 256:COLS], jnp.zeros((LEV, 128 - LAST), F32)], axis=1)

    def roll(a, shift):
        return pltpu.roll(a, shift, 1)

    def fixed(a, shift):
        return a if shift % 128 == 0 else pltpu.roll(a, shift % 128, 1)

    def pack(row, fields=range(NF)):
        for_east = jnp.zeros((LEV, 128), F32)
        for_west = jnp.zeros((LEV, 128), F32)
        for f in fields:
            here = (lane >= 32 * f) & (lane < 32 * f + 32)
            for_east = jnp.where(here, fixed(tile(row, f, 2), 32 * f - (LAST - 32)), for_east)
            for_west = jnp.where(here, fixed(tile(row, f, 0), 32 * f), for_west)
        return for_east, for_west

    def chunk_copy(c, i):
        source, goal, target = ((to_east, from_west, east), (to_west, from_east, west))[i]
        rows = pl.ds(c * CHUNK, CHUNK)
        return pltpu.make_async_remote_copy(
            source.at[rows], goal.at[rows], send_sem.at[i, c], recv_sem.at[i, c],
            device_id=at(target, lat), device_id_type=MESH,
        )

    def corner_copy(i):
        source, goal, target = ((to_east, from_west, east), (to_west, from_east, west))[i]
        rows = pl.ds(ROWS, 2)
        return pltpu.make_async_remote_copy(
            source.at[rows], goal.at[rows], send_sem.at[i, NCHUNK], recv_sem.at[i, NCHUNK],
            device_id=at(target, lat), device_id_type=MESH,
        )

    def x_copy(side):
        source, goal, target = ((x_east, xf_west, east), (x_west, xf_east, west))[side]
        return pltpu.make_async_remote_copy(
            source, goal, x_send.at[side], x_recv.at[side], device_id=at(target, lat), device_id_type=MESH
        )

    def pack_chunk(c, carry):
        xe, xw = carry
        load(c).wait()
        for i in range(CHUNK):
            r = c * CHUNK + i
            to_east[r], to_west[r] = pack(r + 1)
            for slot, f in enumerate((0, 2, 3)):
                goal = 32 * slot + r
                here = lane == goal
                xe = jnp.where(here, roll(tile(r + 1, f, 2), lax.rem(goal + 256 - jnp.where(polar, LAST - 33, LAST - 1), 128)), xe)
                xw = jnp.where(here, roll(tile(r + 1, f, 0), lax.rem(goal + 256 - jnp.where(polar, 32, 0), 128)), xw)

        early_chunk = polar & (c < STAGES[0])

        @pl.when(early_chunk & second[EAST])
        def _():
            chunk_copy(c, 0).start()

        @pl.when(early_chunk & second[WEST])
        def _():
            chunk_copy(c, 1).start()

        return xe, xw

    xe, xw = lax.fori_loop(0, NCHUNK, pack_chunk, (jnp.zeros((LEV, 128), F32),) * 2)
    x_east[...] = xe
    x_west[...] = xw

    def send_stage(stage):
        ends = (0, *STAGES, NCHUNK)
        for i in range(2):
            is_first = first[(EAST, WEST)[i]]
            begin = jnp.where(is_first, ends[stage - 1], ends[stage])
            end = jnp.where(polar, jnp.where(is_first, ends[stage], ends[stage + 1]), begin)

            def send(c, carry):
                chunk_copy(c, i).start()
                return carry

            lax.fori_loop(begin, end, send, 0)

    @pl.when(first[EAST])
    def _():
        pl.semaphore_wait(ready.at[EAST], 1)

    x_copy(0).start()

    @pl.when(first[NORTH] & ~last_south)
    def _():
        pl.semaphore_wait(ready.at[NORTH], 1)
        row_copy(0, north).start()

    @pl.when(first[WEST])
    def _():
        pl.semaphore_wait(ready.at[WEST], 1)

    x_copy(1).start()
    send_stage(1)
    for copy in smalls:
        copy.wait()

    origin = jnp.where(lat < NLAT_DEV // 4, lat * ROWS, jnp.where(polar, lat * ROWS - 256, 0))

    def coefficients(r):
        width = jnp.full((LEV, 128), band[origin + r], jnp.int32).astype(F32) + 1.0
        strength = jnp.full((LEV, 128), jnp.where(polar, damping[origin + r], 0.0), F32)
        return width, 1.0 - strength, strength / (width * width)

    def weights(distances, width):
        top = width.astype(BF16)
        rows, columns = distances.shape
        top = jnp.concatenate([top] * (rows // LEV), axis=0)
        top = jnp.concatenate([top] * (columns // 128), axis=1)
        return jnp.maximum(top - distances[...], jnp.zeros((), BF16))

    def step(r, mid, up, down, diff):
        kx, ky, fs = table[1, r], table[2, r], table[3, r]
        u, v, h, q = (mid(f) for f in range(NF))
        vn, hn, qn = (up(f) for f in (1, 2, 3))
        vs, hs, qs = (down(f) for f in (1, 2, 3))
        flux = vn * hn * table[0, r + 2] - vs * hs * table[0, r]
        d_flux, d_h, d_q = diff
        h_new = h - kx * d_flux - ky * flux
        u_new = u - kx * d_h + fs * v
        v_new = v - KY * (hn - hs) - fs * u
        q_new = q - kx * u * d_q - KY * v * (qn - qs)
        return u_new, v_new, h_new, q_new

    def halves(a):
        high = a.astype(BF16)
        return high, (a - high.astype(F32)).astype(BF16)

    def product(left, right):
        return jnp.dot(left, right, preferred_element_type=F32)

    def early(r):
        row = r + 1
        width, keep, gain = coefficients(r)
        mids = [[tile(row, f, t) for t in range(3)] for f in range(NF)]

        def difference(tiles):
            lo = [roll(a, 127) for a in tiles]
            hi = [roll(a, 1) for a in tiles]
            result = []
            for t in range(3):
                e = lo[t] if t == 2 else jnp.where(lane == 127, lo[t + 1], lo[t])
                w = hi[t] if t == 0 else jnp.where(lane == 0, hi[t - 1], hi[t])
                result.append(e - w)
            return result

        d_flux = difference([mids[0][t] * mids[2][t] for t in range(3)])
        d_h = difference(mids[2])
        d_q = difference(mids[3])
        stepped = []
        for t in range(3):
            values = step(
                r, lambda f: mids[f][t], lambda f: tile(row + 1, f, t), lambda f: tile(row - 1, f, t),
                (d_flux[t], d_h[t], d_q[t]),
            )
            if t == 0:
                values = [jnp.where(lane == 0, 0.0, a) for a in values]
            if t == 2:
                values = [jnp.where(lane >= LAST - 1, 0.0, a) for a in values]
            stepped.append(values)
        right = weights(near, width)
        parts = [[halves(a) for a in values] for values in stepped]
        zero = jnp.zeros((LEV, 128), BF16)

        def left(half):
            blocks = []
            for t in range(3):
                for f in range(NF):
                    after = parts[t + 1][f][half] if t < 2 else zero
                    before = parts[t - 1][f][half] if t > 0 else zero
                    side = jnp.where(lane < 64, after, before)
                    blocks.append(jnp.concatenate([parts[t][f][half], side], axis=1))
            return jnp.concatenate(blocks, axis=0)

        both = product(jnp.concatenate([left(0), left(1)], axis=0), right)
        smooth = both[: both.shape[0] // 2] + both[both.shape[0] // 2 :]
        for t in range(3):
            for f in range(NF):
                place = (t * NF + f) * LEV
                value = keep * stepped[t][f] + gain * smooth[place : place + LEV]
                if t < 2:
                    out[r, f, :, t * 128 : (t + 1) * 128] = value
                else:
                    out[r, f, :, 256:COLS] = value[:, :LAST]

    outer_lanes = (lane == jnp.where(polar, 63, 31)) | (lane == jnp.where(polar, 95, 127))

    def unpack(slot):
        row = lax.rem(slot + 1, ROWS + 2)
        got_west, got_east = from_west[slot], from_east[slot]
        for f in range(NF):
            own = jnp.where(lane < 2, tile(row, f, 0), fixed(tile(row, f, 2), 30 - (LAST - 1)))
            halo = jnp.where(lane >= 96, fixed(got_west, 96 - 32 * f), fixed(got_east, 31 - 32 * f))
            value = jnp.where(lane < 31, own, halo)
            if f != 1:
                outer = roll(x_both[(0, None, 1, 2)[f]], jnp.where(polar, 63, 127) - slot)
                value = jnp.where(outer_lanes, outer, value)
            edge[row, f] = value

    def late(r):
        row = r + 1
        width, keep, gain = coefficients(r)

        def difference(a):
            return roll(a, 127) - roll(a, 1)

        mids = [edge[row, f] for f in range(NF)]
        stepped = step(
            r, lambda f: mids[f], lambda f: edge[row + 1, f], lambda f: edge[row - 1, f],
            (difference(mids[0] * mids[2]), difference(mids[2]), difference(mids[3])),
        )
        right = weights(far, width)
        parts = [halves(a) for a in stepped]
        left = jnp.concatenate([jnp.concatenate(p, axis=1) for p in parts], axis=0)
        smooth = product(left, jnp.concatenate([right, right], axis=0))
        for f in range(NF):
            more = gain * smooth[f * LEV : (f + 1) * LEV, :128] + jnp.where(lane == 0, keep * stepped[f], 0.0)
            out[r, f, :, 0:128] = out[r, f, :, 0:128] + more
            last = roll(stepped[f], LAST - 1 - 30)
            more = gain * smooth[f * LEV : (f + 1) * LEV, 128:] + jnp.where(lane == LAST - 1, keep * last, 0.0)
            out[r, f, :, 256:COLS] = out[r, f, :, 256:COLS] + more[:, :LAST]

    def early_group(g, carry):
        for i in range(GROUP):
            early(lax.rem(g * GROUP + 1 + i, ROWS))
        return carry

    def late_group(g, carry):
        @pl.when(polar)
        def _():
            for side in range(2):
                chunk_copy(2 * g + 1, side).wait()
                chunk_copy(2 * g + 2, side).wait()

        for i in range(GROUP):
            unpack(g * GROUP + 2 + i)
            late(lax.rem(g * GROUP + 1 + i, ROWS))
        return carry

    def outer_rows():
        @pl.when(has_north)
        def _():
            row_copy(1, north).wait_recv()

        @pl.when(has_south)
        def _():
            row_copy(0, south).wait_recv()

        @pl.when(polar)
        def _():
            for i, row in enumerate((ROWS + 1, 0)):
                to_east[ROWS + i], to_west[ROWS + i] = pack(row, (1, 2, 3))
            for side in range(2):
                corner_copy(side).start()

    def outer_early():
        for r in (ROWS - 1, 0):
            early(r)

    lax.fori_loop(0, 1, early_group, 0)
    send_stage(2)
    lax.fori_loop(1, 2, early_group, 0)
    send_stage(3)
    pl.when(~crossing & polar)(outer_rows)
    lax.fori_loop(2, 3, early_group, 0)
    send_stage(4)
    @pl.when(last_south)
    def _():
        pl.semaphore_wait(ready.at[NORTH], 1)
        row_copy(0, north).start()

    @pl.when(first[SOUTH])
    def _():
        pl.semaphore_wait(ready.at[SOUTH], 1)
        row_copy(1, south).start()


    for r in range(3 * GROUP + 1, ROWS - 1):
        early(r)

    pl.when(crossing & polar)(outer_rows)
    pl.when(polar)(outer_early)

    for side in range(2):
        x_copy(side).wait()
    near_x = jnp.where(polar, xf_east[...], xf_west[...])
    far_x = jnp.where(polar, xf_west[...], xf_east[...])
    for slot in range(3):
        x_both[slot] = jnp.where(lane < 32, fixed(near_x, -32 * slot), fixed(far_x, 32 - 32 * slot))

    @pl.when(polar)
    def _():
        for side in range(2):
            chunk_copy(0, side).wait()

    for slot in range(2):
        unpack(slot)
    lax.fori_loop(0, 3, late_group, 0)

    @pl.when(polar)
    def _():
        for side in range(2):
            chunk_copy(NCHUNK - 1, side).wait()

    for r in range(3 * GROUP + 1, ROWS - 1):
        unpack(r + 1)
        late(r)

    @pl.when(~polar)
    def _():
        outer_rows()
        outer_early()

    @pl.when(polar)
    def _():
        for side in range(2):
            corner_copy(side).wait()

    unpack(ROWS)
    unpack(ROWS + 1)
    late(ROWS - 1)
    late(0)

    @pl.when(has_north)
    def _():
        row_copy(0, north).wait_send()

    @pl.when(has_south)
    def _():
        row_copy(1, south).wait_send()


def shards(state, band, damping):
    hbm = pl.BlockSpec(memory_space=pltpu.HBM)
    packed = pltpu.VMEM((ROWS + 2, LEV, 128), F32)
    extra = pltpu.VMEM((LEV, 128), F32)
    dma = pltpu.SemaphoreType.DMA
    return pl.pallas_call(
        kernel,
        out_shape=pltpu.VMEM(state.shape, F32),
        in_specs=[hbm] * 4,
        out_specs=pl.BlockSpec(memory_space=pltpu.VMEM),
        scratch_shapes=[
            pltpu.VMEM((ROWS + 2, NF, LEV, COLS), F32),
            packed, packed, packed, packed,
            extra, extra, extra, extra,
            pltpu.VMEM((3, LEV, 128), F32),
            pltpu.VMEM((ROWS + 2, NF, LEV, 128), F32),
            pltpu.VMEM((256, 128), BF16),
            pltpu.VMEM((128, 256), BF16),
            pltpu.SMEM((256,), jnp.int32),
            pltpu.SMEM((256,), F32),
            pltpu.SMEM((8, 128), F32),
            dma((NCHUNK,)), dma((3,)),
            dma((2, NCHUNK + 1)), dma((2, NCHUNK + 1)),
            dma((2,)), dma((2,)),
            dma((2,)), dma((2,)),
            pltpu.SemaphoreType.REGULAR((4,)),
        ],
        compiler_params=pltpu.CompilerParams(
            collective_id=0, has_side_effects=True, vmem_limit_bytes=60 * 1024 * 1024
        ),
    )(state, band, damping, jnp.asarray(row_table()))


def solution(mesh):
    in_specs = (P("lat", None, None, "lon"), P(), P())
    out_specs = P("lat", None, None, "lon")
    return jax.shard_map(shards, mesh=mesh, in_specs=in_specs, out_specs=out_specs, check_vma=False)
```

```python
import functools
import math

import jax
import jax.numpy as jnp
import numpy as np
from jax import lax
from jax.experimental import pallas as pl
from jax.experimental.pallas import tpu as pltpu
from jax.sharding import PartitionSpec as P

MAXB = 32
KX = 0.004
KY = 0.1
FC = 0.2

NLON_DEV = 8
NLAT_DEV = 16
NX = 4
ROWS = 32
NF = 4
LEV = 16
COLS = 360
LAST = COLS - 256
CHUNK = 4
NCHUNK = ROWS // CHUNK
STAGES = (3, 5, 7, 8)
GROUP = 8
MESH = pl.DeviceIdType.MESH
F32 = jnp.float32
BF16 = jnp.bfloat16


def row_table():
    total = ROWS * NLAT_DEV
    rows = np.arange(-1, total + 1, dtype=np.float32)
    angle = np.float32(math.pi) * ((rows + np.float32(0.5)) / np.float32(total) - np.float32(0.5))
    cos = np.cos(angle.astype(np.float64)).astype(np.float32)
    sin = np.sin(angle.astype(np.float64)).astype(np.float32)
    inv = np.float32(1.0) / cos
    table = np.zeros((NLAT_DEV, 8, 128), np.float32)
    for lat in range(NLAT_DEV):
        pad = slice(lat * ROWS, lat * ROWS + ROWS + 2)
        mid = slice(lat * ROWS + 1, lat * ROWS + ROWS + 1)
        table[lat, 0, : ROWS + 2] = cos[pad]
        table[lat, 1, :ROWS] = np.float32(KX) * inv[mid]
        table[lat, 2, :ROWS] = np.float32(KY) * inv[mid]
        table[lat, 3, :ROWS] = np.float32(FC) * sin[mid]
    return table


def kernel(
    state, band_hbm, damping_hbm, table_hbm, out,
    buf, to_east, to_west, from_west, from_east, x_east, x_west, xf_west, xf_east, x_both,
    edge, near, far, band, damping, table,
    load_sem, small_sem, send_sem, recv_sem, row_send, row_recv, x_send, x_recv, ready,
):
    lon, lat = lax.axis_index("lon"), lax.axis_index("lat")
    east, west = lax.rem(lon + 1, NLON_DEV), lax.rem(lon + NLON_DEV - 1, NLON_DEV)
    north, south = lax.rem(lat + 1, NLAT_DEV), lax.rem(lat + NLAT_DEV - 1, NLAT_DEV)
    has_north, has_south = lat < NLAT_DEV - 1, lat > 0
    x = lax.rem(lat, NX)
    polar = (lat < NLAT_DEV // 4) | (lat >= NLAT_DEV - NLAT_DEV // 4)
    crossing = ((x == NX - 1) & has_north) | ((x == 0) & has_south)
    last_south, first_mid = lat == NLAT_DEV // 4 - 1, lat == NLAT_DEV // 4
    first = ((x < NX - 1) | last_south, (x == 0) & has_south & ~first_mid, lon < NLON_DEV - 1, lon == 0)
    second = ((x == NX - 1) & has_north & ~last_south, (x > 0) | first_mid, lon == NLON_DEV - 1, lon > 0)
    others = ((lon, north), (lon, south), (east, lat), (west, lat))
    NORTH, SOUTH, EAST, WEST = range(4)
    OPPOSITE = (SOUTH, NORTH, WEST, EAST)

    def at(a, b):
        return {"lon": a, "lat": b}

    def load(c):
        rows = pl.ds(c * CHUNK, CHUNK)
        return pltpu.make_async_copy(
            state.at[rows], buf.at[pl.ds(c * CHUNK + 1, CHUNK)], load_sem.at[c]
        )

    smalls = [
        pltpu.make_async_copy(band_hbm, band, small_sem.at[0]),
        pltpu.make_async_copy(damping_hbm, damping, small_sem.at[1]),
        pltpu.make_async_copy(table_hbm.at[lat], table, small_sem.at[2]),
    ]
    for c in range(NCHUNK):
        load(c).start()
    for copy in smalls:
        copy.start()

    barrier = pltpu.get_barrier_semaphore()
    for side in range(4):

        @pl.when(first[side])
        def _():
            pl.semaphore_signal(barrier, 1, device_id=at(*others[side]), device_id_type=MESH)

    @pl.when(lon == 1)
    def _():
        pl.semaphore_signal(barrier, 1, device_id=at(west, lat), device_id_type=MESH)

    k = lax.broadcasted_iota(jnp.int32, (256, 128), 0)
    n = lax.broadcasted_iota(jnp.int32, (256, 128), 1)
    place = jnp.where(k < 192, k, k - 256)
    near[...] = jnp.minimum(jnp.abs(place - n), 255).astype(F32).astype(BF16)
    k = lax.broadcasted_iota(jnp.int32, (128, 256), 0)
    n = lax.broadcasted_iota(jnp.int32, (128, 256), 1)
    place = jnp.where(k >= 96, k - 128, jnp.where(k == 0, 0, jnp.where((k >= 30) & (k < 63), k + 329, 10000)))
    column = jnp.where(n < 128, n, n + 128)
    far[...] = jnp.minimum(jnp.abs(place - column), 255).astype(F32).astype(BF16)

    @pl.when(~has_south)
    def _():
        buf[0, 1:4] = jnp.zeros((3, LEV, COLS), F32)

    @pl.when(~has_north)
    def _():
        buf[ROWS + 1, 1:4] = jnp.zeros((3, LEV, COLS), F32)

    @pl.when(~polar)
    def _():
        from_west[...] = jnp.zeros(from_west.shape, F32)
        from_east[...] = jnp.zeros(from_east.shape, F32)

    pl.semaphore_wait(barrier, sum(jnp.where(flag, 1, 0) for flag in (*second, lon == 0)))

    def row_copy(i, target):
        source = state.at[ROWS - 1 if i == 0 else 0, pl.ds(1, 3)]
        goal = buf.at[0 if i == 0 else ROWS + 1, pl.ds(1, 3)]
        return pltpu.make_async_remote_copy(
            source, goal, row_send.at[i], row_recv.at[i], device_id=at(lon, target), device_id_type=MESH
        )

    @pl.when(second[SOUTH])
    def _():
        row_copy(1, south).start()

    @pl.when(second[NORTH])
    def _():
        row_copy(0, north).start()

    for side in range(4):

        @pl.when(second[side])
        def _():
            pl.semaphore_signal(ready.at[OPPOSITE[side]], 1, device_id=at(*others[side]), device_id_type=MESH)

    lane = lax.broadcasted_iota(jnp.int32, (LEV, 128), 1)

    def tile(row, field, t):
        if t < 2:
            return buf[row, field, :, t * 128 : (t + 1) * 128]
        return jnp.concatenate([buf[row, field, :, 256:COLS], jnp.zeros((LEV, 128 - LAST), F32)], axis=1)

    def roll(a, shift):
        return pltpu.roll(a, shift, 1)

    def fixed(a, shift):
        return a if shift % 128 == 0 else pltpu.roll(a, shift % 128, 1)

    def pack(row, fields=range(NF)):
        for_east = jnp.zeros((LEV, 128), F32)
        for_west = jnp.zeros((LEV, 128), F32)
        for f in fields:
            here = (lane >= 32 * f) & (lane < 32 * f + 32)
            for_east = jnp.where(here, fixed(tile(row, f, 2), 32 * f - (LAST - 32)), for_east)
            for_west = jnp.where(here, fixed(tile(row, f, 0), 32 * f), for_west)
        return for_east, for_west

    def chunk_copy(c, i):
        source, goal, target = ((to_east, from_west, east), (to_west, from_east, west))[i]
        rows = pl.ds(c * CHUNK, CHUNK)
        return pltpu.make_async_remote_copy(
            source.at[rows], goal.at[rows], send_sem.at[i, c], recv_sem.at[i, c],
            device_id=at(target, lat), device_id_type=MESH,
        )

    def corner_copy(i):
        source, goal, target = ((to_east, from_west, east), (to_west, from_east, west))[i]
        rows = pl.ds(ROWS, 2)
        return pltpu.make_async_remote_copy(
            source.at[rows], goal.at[rows], send_sem.at[i, NCHUNK], recv_sem.at[i, NCHUNK],
            device_id=at(target, lat), device_id_type=MESH,
        )

    def x_copy(side):
        source, goal, target = ((x_east, xf_west, east), (x_west, xf_east, west))[side]
        return pltpu.make_async_remote_copy(
            source, goal, x_send.at[side], x_recv.at[side], device_id=at(target, lat), device_id_type=MESH
        )

    def pack_chunk(c, carry):
        xe, xw = carry
        load(c).wait()
        for i in range(CHUNK):
            r = c * CHUNK + i
            to_east[r], to_west[r] = pack(r + 1)
            for slot, f in enumerate((0, 2, 3)):
                goal = 32 * slot + r
                here = lane == goal
                xe = jnp.where(here, roll(tile(r + 1, f, 2), lax.rem(goal + 256 - jnp.where(polar, LAST - 33, LAST - 1), 128)), xe)
                xw = jnp.where(here, roll(tile(r + 1, f, 0), lax.rem(goal + 256 - jnp.where(polar, 32, 0), 128)), xw)

        early_chunk = polar & (c < STAGES[0])

        @pl.when(early_chunk & second[EAST])
        def _():
            chunk_copy(c, 0).start()

        @pl.when(early_chunk & second[WEST])
        def _():
            chunk_copy(c, 1).start()

        return xe, xw

    xe, xw = lax.fori_loop(0, NCHUNK, pack_chunk, (jnp.zeros((LEV, 128), F32),) * 2)
    x_east[...] = xe
    x_west[...] = xw

    def send_stage(stage):
        ends = (0, *STAGES, NCHUNK)
        for i in range(2):
            is_first = first[(EAST, WEST)[i]]
            begin = jnp.where(is_first, ends[stage - 1], ends[stage])
            end = jnp.where(polar, jnp.where(is_first, ends[stage], ends[stage + 1]), begin)

            def send(c, carry):
                chunk_copy(c, i).start()
                return carry

            lax.fori_loop(begin, end, send, 0)

    @pl.when(first[EAST])
    def _():
        pl.semaphore_wait(ready.at[EAST], 1)

    x_copy(0).start()

    @pl.when(first[NORTH] & ~last_south)
    def _():
        pl.semaphore_wait(ready.at[NORTH], 1)
        row_copy(0, north).start()

    @pl.when(first[WEST])
    def _():
        pl.semaphore_wait(ready.at[WEST], 1)

    x_copy(1).start()
    send_stage(1)
    for copy in smalls:
        copy.wait()

    origin = jnp.where(lat < NLAT_DEV // 4, lat * ROWS, jnp.where(polar, lat * ROWS - 256, 0))

    def coefficients(r):
        width = jnp.full((LEV, 128), band[origin + r], jnp.int32).astype(F32) + 1.0
        strength = jnp.full((LEV, 128), jnp.where(polar, damping[origin + r], 0.0), F32)
        return width, 1.0 - strength, strength / (width * width)

    def weights(distances, width):
        top = width.astype(BF16)
        rows, columns = distances.shape
        top = jnp.concatenate([top] * (rows // LEV), axis=0)
        top = jnp.concatenate([top] * (columns // 128), axis=1)
        return jnp.maximum(top - distances[...], jnp.zeros((), BF16))

    def step(r, mid, up, down, diff):
        kx, ky, fs = table[1, r], table[2, r], table[3, r]
        u, v, h, q = (mid(f) for f in range(NF))
        vn, hn, qn = (up(f) for f in (1, 2, 3))
        vs, hs, qs = (down(f) for f in (1, 2, 3))
        flux = vn * hn * table[0, r + 2] - vs * hs * table[0, r]
        d_flux, d_h, d_q = diff
        h_new = h - kx * d_flux - ky * flux
        u_new = u - kx * d_h + fs * v
        v_new = v - KY * (hn - hs) - fs * u
        q_new = q - kx * u * d_q - KY * v * (qn - qs)
        return u_new, v_new, h_new, q_new

    def halves(a):
        high = a.astype(BF16)
        return high, (a - high.astype(F32)).astype(BF16)

    def product(left, right):
        return jnp.dot(left, right, preferred_element_type=F32)

    def early(r):
        row = r + 1
        width, keep, gain = coefficients(r)
        mids = [[tile(row, f, t) for t in range(3)] for f in range(NF)]

        def difference(tiles):
            lo = [roll(a, 127) for a in tiles]
            hi = [roll(a, 1) for a in tiles]
            result = []
            for t in range(3):
                e = lo[t] if t == 2 else jnp.where(lane == 127, lo[t + 1], lo[t])
                w = hi[t] if t == 0 else jnp.where(lane == 0, hi[t - 1], hi[t])
                result.append(e - w)
            return result

        d_flux = difference([mids[0][t] * mids[2][t] for t in range(3)])
        d_h = difference(mids[2])
        d_q = difference(mids[3])
        stepped = []
        for t in range(3):
            values = step(
                r, lambda f: mids[f][t], lambda f: tile(row + 1, f, t), lambda f: tile(row - 1, f, t),
                (d_flux[t], d_h[t], d_q[t]),
            )
            if t == 0:
                values = [jnp.where(lane == 0, 0.0, a) for a in values]
            if t == 2:
                values = [jnp.where(lane >= LAST - 1, 0.0, a) for a in values]
            stepped.append(values)
        right = weights(near, width)
        parts = [[halves(a) for a in values] for values in stepped]
        zero = jnp.zeros((LEV, 128), BF16)

        def left(half):
            blocks = []
            for t in range(3):
                for f in range(NF):
                    after = parts[t + 1][f][half] if t < 2 else zero
                    before = parts[t - 1][f][half] if t > 0 else zero
                    side = jnp.where(lane < 64, after, before)
                    blocks.append(jnp.concatenate([parts[t][f][half], side], axis=1))
            return jnp.concatenate(blocks, axis=0)

        both = product(jnp.concatenate([left(0), left(1)], axis=0), right)
        smooth = both[: both.shape[0] // 2] + both[both.shape[0] // 2 :]
        for t in range(3):
            for f in range(NF):
                place = (t * NF + f) * LEV
                value = keep * stepped[t][f] + gain * smooth[place : place + LEV]
                if t < 2:
                    out[r, f, :, t * 128 : (t + 1) * 128] = value
                else:
                    out[r, f, :, 256:COLS] = value[:, :LAST]

    outer_lanes = (lane == jnp.where(polar, 63, 31)) | (lane == jnp.where(polar, 95, 127))

    def unpack(slot):
        row = lax.rem(slot + 1, ROWS + 2)
        got_west, got_east = from_west[slot], from_east[slot]
        for f in range(NF):
            own = jnp.where(lane < 2, tile(row, f, 0), fixed(tile(row, f, 2), 30 - (LAST - 1)))
            halo = jnp.where(lane >= 96, fixed(got_west, 96 - 32 * f), fixed(got_east, 31 - 32 * f))
            value = jnp.where(lane < 31, own, halo)
            if f != 1:
                outer = roll(x_both[(0, None, 1, 2)[f]], jnp.where(polar, 63, 127) - slot)
                value = jnp.where(outer_lanes, outer, value)
            edge[row, f] = value

    def late(r):
        row = r + 1
        width, keep, gain = coefficients(r)

        def difference(a):
            return roll(a, 127) - roll(a, 1)

        mids = [edge[row, f] for f in range(NF)]
        stepped = step(
            r, lambda f: mids[f], lambda f: edge[row + 1, f], lambda f: edge[row - 1, f],
            (difference(mids[0] * mids[2]), difference(mids[2]), difference(mids[3])),
        )
        right = weights(far, width)
        parts = [halves(a) for a in stepped]
        left = jnp.concatenate([jnp.concatenate(p, axis=1) for p in parts], axis=0)
        smooth = product(left, jnp.concatenate([right, right], axis=0))
        for f in range(NF):
            more = gain * smooth[f * LEV : (f + 1) * LEV, :128] + jnp.where(lane == 0, keep * stepped[f], 0.0)
            out[r, f, :, 0:128] = out[r, f, :, 0:128] + more
            last = roll(stepped[f], LAST - 1 - 30)
            more = gain * smooth[f * LEV : (f + 1) * LEV, 128:] + jnp.where(lane == LAST - 1, keep * last, 0.0)
            out[r, f, :, 256:COLS] = out[r, f, :, 256:COLS] + more[:, :LAST]

    def early_group(g, carry):
        for i in range(GROUP):
            early(lax.rem(g * GROUP + 1 + i, ROWS))
        return carry

    def late_group(g, carry):
        @pl.when(polar)
        def _():
            for side in range(2):
                chunk_copy(2 * g + 1, side).wait()
                chunk_copy(2 * g + 2, side).wait()

        for i in range(GROUP):
            unpack(g * GROUP + 2 + i)
            late(lax.rem(g * GROUP + 1 + i, ROWS))
        return carry

    def outer_rows():
        @pl.when(has_north)
        def _():
            row_copy(1, north).wait_recv()

        @pl.when(has_south)
        def _():
            row_copy(0, south).wait_recv()

        @pl.when(polar)
        def _():
            for i, row in enumerate((ROWS + 1, 0)):
                to_east[ROWS + i], to_west[ROWS + i] = pack(row, (1, 2, 3))
            for side in range(2):
                corner_copy(side).start()

    def crossing_send():
        @pl.when(last_south)
        def _():
            pl.semaphore_wait(ready.at[NORTH], 1)
            row_copy(0, north).start()

        @pl.when(first[SOUTH])
        def _():
            pl.semaphore_wait(ready.at[SOUTH], 1)
            row_copy(1, south).start()

    soon = polar & ~crossing & (lon == NLON_DEV - 1)

    def outer_early():
        for r in (ROWS - 1, 0):
            early(r)

    lax.fori_loop(0, 1, early_group, 0)
    send_stage(2)
    lax.fori_loop(1, 2, early_group, 0)
    send_stage(3)
    pl.when(soon)(outer_rows)
    pl.when(lon < 2)(crossing_send)
    lax.fori_loop(2, 3, early_group, 0)
    send_stage(4)
    pl.when(lon >= 2)(crossing_send)

    for r in range(3 * GROUP + 1, ROWS - 1):
        early(r)

    pl.when(polar & ~soon)(outer_rows)
    pl.when(polar)(outer_early)

    for side in range(2):
        x_copy(side).wait()
    near_x = jnp.where(polar, xf_east[...], xf_west[...])
    far_x = jnp.where(polar, xf_west[...], xf_east[...])
    for slot in range(3):
        x_both[slot] = jnp.where(lane < 32, fixed(near_x, -32 * slot), fixed(far_x, 32 - 32 * slot))

    @pl.when(polar)
    def _():
        for side in range(2):
            chunk_copy(0, side).wait()

    for slot in range(2):
        unpack(slot)
    lax.fori_loop(0, 3, late_group, 0)

    @pl.when(polar)
    def _():
        for side in range(2):
            chunk_copy(NCHUNK - 1, side).wait()

    for r in range(3 * GROUP + 1, ROWS - 1):
        unpack(r + 1)
        late(r)

    @pl.when(~polar)
    def _():
        outer_rows()
        outer_early()

    @pl.when(polar)
    def _():
        for side in range(2):
            corner_copy(side).wait()

    unpack(ROWS)
    unpack(ROWS + 1)
    late(ROWS - 1)
    late(0)

    @pl.when(has_north)
    def _():
        row_copy(0, north).wait_send()

    @pl.when(has_south)
    def _():
        row_copy(1, south).wait_send()


def shards(state, band, damping):
    hbm = pl.BlockSpec(memory_space=pltpu.HBM)
    packed = pltpu.VMEM((ROWS + 2, LEV, 128), F32)
    extra = pltpu.VMEM((LEV, 128), F32)
    dma = pltpu.SemaphoreType.DMA
    return pl.pallas_call(
        kernel,
        out_shape=pltpu.VMEM(state.shape, F32),
        in_specs=[hbm] * 4,
        out_specs=pl.BlockSpec(memory_space=pltpu.VMEM),
        scratch_shapes=[
            pltpu.VMEM((ROWS + 2, NF, LEV, COLS), F32),
            packed, packed, packed, packed,
            extra, extra, extra, extra,
            pltpu.VMEM((3, LEV, 128), F32),
            pltpu.VMEM((ROWS + 2, NF, LEV, 128), F32),
            pltpu.VMEM((256, 128), BF16),
            pltpu.VMEM((128, 256), BF16),
            pltpu.SMEM((256,), jnp.int32),
            pltpu.SMEM((256,), F32),
            pltpu.SMEM((8, 128), F32),
            dma((NCHUNK,)), dma((3,)),
            dma((2, NCHUNK + 1)), dma((2, NCHUNK + 1)),
            dma((2,)), dma((2,)),
            dma((2,)), dma((2,)),
            pltpu.SemaphoreType.REGULAR((4,)),
        ],
        compiler_params=pltpu.CompilerParams(
            collective_id=0, has_side_effects=True, vmem_limit_bytes=60 * 1024 * 1024
        ),
    )(state, band, damping, jnp.asarray(row_table()))


def solution(mesh):
    in_specs = (P("lat", None, None, "lon"), P(), P())
    out_specs = P("lat", None, None, "lon")
    return jax.shard_map(shards, mesh=mesh, in_specs=in_specs, out_specs=out_specs, check_vma=False)
```

```python
import functools
import math

import jax
import jax.numpy as jnp
import numpy as np
from jax import lax
from jax.experimental import pallas as pl
from jax.experimental.pallas import tpu as pltpu
from jax.sharding import PartitionSpec as P

MAXB = 32
KX = 0.004
KY = 0.1
FC = 0.2

NLON_DEV = 8
NLAT_DEV = 16
NX = 4
ROWS = 32
NF = 4
LEV = 16
COLS = 360
LAST = COLS - 256
CHUNK = 4
NCHUNK = ROWS // CHUNK
STAGES = (3, 5, 7, 8)
GROUP = 8
MESH = pl.DeviceIdType.MESH
F32 = jnp.float32
BF16 = jnp.bfloat16


def row_table():
    total = ROWS * NLAT_DEV
    rows = np.arange(-1, total + 1, dtype=np.float32)
    angle = np.float32(math.pi) * ((rows + np.float32(0.5)) / np.float32(total) - np.float32(0.5))
    cos = np.cos(angle.astype(np.float64)).astype(np.float32)
    sin = np.sin(angle.astype(np.float64)).astype(np.float32)
    inv = np.float32(1.0) / cos
    table = np.zeros((NLAT_DEV, 8, 128), np.float32)
    for lat in range(NLAT_DEV):
        pad = slice(lat * ROWS, lat * ROWS + ROWS + 2)
        mid = slice(lat * ROWS + 1, lat * ROWS + ROWS + 1)
        table[lat, 0, : ROWS + 2] = cos[pad]
        table[lat, 1, :ROWS] = np.float32(KX) * inv[mid]
        table[lat, 2, :ROWS] = np.float32(KY) * inv[mid]
        table[lat, 3, :ROWS] = np.float32(FC) * sin[mid]
    return table


def kernel(
    state, band_hbm, damping_hbm, table_hbm, out,
    buf, to_east, to_west, from_west, from_east, x_east, x_west, xf_west, xf_east, x_both,
    edge, near, far, band, damping, table,
    load_sem, small_sem, send_sem, recv_sem, row_send, row_recv, x_send, x_recv, ready,
):
    lon, lat = lax.axis_index("lon"), lax.axis_index("lat")
    east, west = lax.rem(lon + 1, NLON_DEV), lax.rem(lon + NLON_DEV - 1, NLON_DEV)
    north, south = lax.rem(lat + 1, NLAT_DEV), lax.rem(lat + NLAT_DEV - 1, NLAT_DEV)
    has_north, has_south = lat < NLAT_DEV - 1, lat > 0
    x = lax.rem(lat, NX)
    polar = (lat < NLAT_DEV // 4) | (lat >= NLAT_DEV - NLAT_DEV // 4)
    crossing = ((x == NX - 1) & has_north) | ((x == 0) & has_south)
    last_south, first_mid = lat == NLAT_DEV // 4 - 1, lat == NLAT_DEV // 4
    first = ((x < NX - 1) | last_south, (x == 0) & has_south & ~first_mid, lon < NLON_DEV - 1, lon == 0)
    second = ((x == NX - 1) & has_north & ~last_south, (x > 0) | first_mid, lon == NLON_DEV - 1, lon > 0)
    others = ((lon, north), (lon, south), (east, lat), (west, lat))
    NORTH, SOUTH, EAST, WEST = range(4)
    OPPOSITE = (SOUTH, NORTH, WEST, EAST)

    def at(a, b):
        return {"lon": a, "lat": b}

    def load(c):
        rows = pl.ds(c * CHUNK, CHUNK)
        return pltpu.make_async_copy(
            state.at[rows], buf.at[pl.ds(c * CHUNK + 1, CHUNK)], load_sem.at[c]
        )

    smalls = [
        pltpu.make_async_copy(band_hbm, band, small_sem.at[0]),
        pltpu.make_async_copy(damping_hbm, damping, small_sem.at[1]),
        pltpu.make_async_copy(table_hbm.at[lat], table, small_sem.at[2]),
    ]
    for c in range(NCHUNK):
        load(c).start()
    for copy in smalls:
        copy.start()

    barrier = pltpu.get_barrier_semaphore()
    for side in range(4):

        @pl.when(first[side])
        def _():
            pl.semaphore_signal(barrier, 1, device_id=at(*others[side]), device_id_type=MESH)

    @pl.when(lon == 1)
    def _():
        pl.semaphore_signal(barrier, 1, device_id=at(west, lat), device_id_type=MESH)

    k = lax.broadcasted_iota(jnp.int32, (256, 128), 0)
    n = lax.broadcasted_iota(jnp.int32, (256, 128), 1)
    place = jnp.where(k < 192, k, k - 256)
    near[...] = jnp.minimum(jnp.abs(place - n), 255).astype(F32).astype(BF16)
    k = lax.broadcasted_iota(jnp.int32, (128, 256), 0)
    n = lax.broadcasted_iota(jnp.int32, (128, 256), 1)
    place = jnp.where(k >= 96, k - 128, jnp.where(k == 0, 0, jnp.where((k >= 30) & (k < 63), k + 329, 10000)))
    column = jnp.where(n < 128, n, n + 128)
    far[...] = jnp.minimum(jnp.abs(place - column), 255).astype(F32).astype(BF16)

    @pl.when(~has_south)
    def _():
        buf[0, 1:4] = jnp.zeros((3, LEV, COLS), F32)

    @pl.when(~has_north)
    def _():
        buf[ROWS + 1, 1:4] = jnp.zeros((3, LEV, COLS), F32)

    @pl.when(~polar)
    def _():
        from_west[...] = jnp.zeros(from_west.shape, F32)
        from_east[...] = jnp.zeros(from_east.shape, F32)

    pl.semaphore_wait(barrier, sum(jnp.where(flag, 1, 0) for flag in (*second, lon == 0)))

    def row_copy(i, target):
        source = state.at[ROWS - 1 if i == 0 else 0, pl.ds(1, 3)]
        goal = buf.at[0 if i == 0 else ROWS + 1, pl.ds(1, 3)]
        return pltpu.make_async_remote_copy(
            source, goal, row_send.at[i], row_recv.at[i], device_id=at(lon, target), device_id_type=MESH
        )

    @pl.when(second[SOUTH])
    def _():
        row_copy(1, south).start()

    @pl.when(second[NORTH])
    def _():
        row_copy(0, north).start()

    for side in range(4):

        @pl.when(second[side])
        def _():
            pl.semaphore_signal(ready.at[OPPOSITE[side]], 1, device_id=at(*others[side]), device_id_type=MESH)

    lane = lax.broadcasted_iota(jnp.int32, (LEV, 128), 1)

    def tile(row, field, t):
        if t < 2:
            return buf[row, field, :, t * 128 : (t + 1) * 128]
        return jnp.concatenate([buf[row, field, :, 256:COLS], jnp.zeros((LEV, 128 - LAST), F32)], axis=1)

    def roll(a, shift):
        return pltpu.roll(a, shift, 1)

    def fixed(a, shift):
        return a if shift % 128 == 0 else pltpu.roll(a, shift % 128, 1)

    def pack(row, fields=range(NF)):
        for_east = jnp.zeros((LEV, 128), F32)
        for_west = jnp.zeros((LEV, 128), F32)
        for f in fields:
            here = (lane >= 32 * f) & (lane < 32 * f + 32)
            for_east = jnp.where(here, fixed(tile(row, f, 2), 32 * f - (LAST - 32)), for_east)
            for_west = jnp.where(here, fixed(tile(row, f, 0), 32 * f), for_west)
        return for_east, for_west

    def chunk_copy(c, i):
        source, goal, target = ((to_east, from_west, east), (to_west, from_east, west))[i]
        rows = pl.ds(c * CHUNK, CHUNK)
        return pltpu.make_async_remote_copy(
            source.at[rows], goal.at[rows], send_sem.at[i, c], recv_sem.at[i, c],
            device_id=at(target, lat), device_id_type=MESH,
        )

    def corner_copy(i):
        source, goal, target = ((to_east, from_west, east), (to_west, from_east, west))[i]
        rows = pl.ds(ROWS, 2)
        return pltpu.make_async_remote_copy(
            source.at[rows], goal.at[rows], send_sem.at[i, NCHUNK], recv_sem.at[i, NCHUNK],
            device_id=at(target, lat), device_id_type=MESH,
        )

    def x_copy(side):
        source, goal, target = ((x_east, xf_west, east), (x_west, xf_east, west))[side]
        return pltpu.make_async_remote_copy(
            source, goal, x_send.at[side], x_recv.at[side], device_id=at(target, lat), device_id_type=MESH
        )

    def pack_chunk(c, carry):
        xe, xw = carry
        load(c).wait()
        for i in range(CHUNK):
            r = c * CHUNK + i
            to_east[r], to_west[r] = pack(r + 1)
            for slot, f in enumerate((0, 2, 3)):
                goal = 32 * slot + r
                here = lane == goal
                xe = jnp.where(here, roll(tile(r + 1, f, 2), lax.rem(goal + 256 - jnp.where(polar, LAST - 33, LAST - 1), 128)), xe)
                xw = jnp.where(here, roll(tile(r + 1, f, 0), lax.rem(goal + 256 - jnp.where(polar, 32, 0), 128)), xw)

        early_chunk = polar & (c < STAGES[0])

        @pl.when(early_chunk & second[EAST])
        def _():
            chunk_copy(c, 0).start()

        @pl.when(early_chunk & second[WEST])
        def _():
            chunk_copy(c, 1).start()

        return xe, xw

    xe, xw = lax.fori_loop(0, NCHUNK, pack_chunk, (jnp.zeros((LEV, 128), F32),) * 2)
    x_east[...] = xe
    x_west[...] = xw

    def send_stage(stage):
        ends = (0, *STAGES, NCHUNK)
        for i in range(2):
            is_first = first[(EAST, WEST)[i]]
            begin = jnp.where(is_first, ends[stage - 1], ends[stage])
            end = jnp.where(polar, jnp.where(is_first, ends[stage], ends[stage + 1]), begin)

            def send(c, carry):
                chunk_copy(c, i).start()
                return carry

            lax.fori_loop(begin, end, send, 0)

    @pl.when(first[EAST])
    def _():
        pl.semaphore_wait(ready.at[EAST], 1)

    x_copy(0).start()

    @pl.when(first[NORTH] & ~last_south)
    def _():
        pl.semaphore_wait(ready.at[NORTH], 1)
        row_copy(0, north).start()

    @pl.when(first[WEST])
    def _():
        pl.semaphore_wait(ready.at[WEST], 1)

    x_copy(1).start()
    send_stage(1)
    for copy in smalls:
        copy.wait()

    origin = jnp.where(lat < NLAT_DEV // 4, lat * ROWS, jnp.where(polar, lat * ROWS - 256, 0))

    def coefficients(r):
        width = jnp.full((LEV, 128), band[origin + r], jnp.int32).astype(F32) + 1.0
        strength = jnp.full((LEV, 128), jnp.where(polar, damping[origin + r], 0.0), F32)
        return width, 1.0 - strength, strength / (width * width)

    def weights(distances, width):
        top = width.astype(BF16)
        rows, columns = distances.shape
        top = jnp.concatenate([top] * (rows // LEV), axis=0)
        top = jnp.concatenate([top] * (columns // 128), axis=1)
        return jnp.maximum(top - distances[...], jnp.zeros((), BF16))

    def step(r, mid, up, down, diff):
        kx, ky, fs = table[1, r], table[2, r], table[3, r]
        u, v, h, q = (mid(f) for f in range(NF))
        vn, hn, qn = (up(f) for f in (1, 2, 3))
        vs, hs, qs = (down(f) for f in (1, 2, 3))
        flux = vn * hn * table[0, r + 2] - vs * hs * table[0, r]
        d_flux, d_h, d_q = diff
        h_new = h - kx * d_flux - ky * flux
        u_new = u - kx * d_h + fs * v
        v_new = v - KY * (hn - hs) - fs * u
        q_new = q - kx * u * d_q - KY * v * (qn - qs)
        return u_new, v_new, h_new, q_new

    def halves(a):
        high = a.astype(BF16)
        return high, (a - high.astype(F32)).astype(BF16)

    def product(left, right):
        return jnp.dot(left, right, preferred_element_type=F32)

    def early(r):
        row = r + 1
        width, keep, gain = coefficients(r)
        mids = [[tile(row, f, t) for t in range(3)] for f in range(NF)]

        def difference(tiles):
            lo = [roll(a, 127) for a in tiles]
            hi = [roll(a, 1) for a in tiles]
            result = []
            for t in range(3):
                e = lo[t] if t == 2 else jnp.where(lane == 127, lo[t + 1], lo[t])
                w = hi[t] if t == 0 else jnp.where(lane == 0, hi[t - 1], hi[t])
                result.append(e - w)
            return result

        d_flux = difference([mids[0][t] * mids[2][t] for t in range(3)])
        d_h = difference(mids[2])
        d_q = difference(mids[3])
        stepped = []
        for t in range(3):
            values = step(
                r, lambda f: mids[f][t], lambda f: tile(row + 1, f, t), lambda f: tile(row - 1, f, t),
                (d_flux[t], d_h[t], d_q[t]),
            )
            if t == 0:
                values = [jnp.where(lane == 0, 0.0, a) for a in values]
            if t == 2:
                values = [jnp.where(lane >= LAST - 1, 0.0, a) for a in values]
            stepped.append(values)
        right = weights(near, width)
        parts = [[halves(a) for a in values] for values in stepped]
        zero = jnp.zeros((LEV, 128), BF16)

        def left(half):
            blocks = []
            for t in range(3):
                for f in range(NF):
                    after = parts[t + 1][f][half] if t < 2 else zero
                    before = parts[t - 1][f][half] if t > 0 else zero
                    side = jnp.where(lane < 64, after, before)
                    blocks.append(jnp.concatenate([parts[t][f][half], side], axis=1))
            return jnp.concatenate(blocks, axis=0)

        both = product(jnp.concatenate([left(0), left(1)], axis=0), right)
        smooth = both[: both.shape[0] // 2] + both[both.shape[0] // 2 :]
        for t in range(3):
            for f in range(NF):
                place = (t * NF + f) * LEV
                value = keep * stepped[t][f] + gain * smooth[place : place + LEV]
                if t < 2:
                    out[r, f, :, t * 128 : (t + 1) * 128] = value
                else:
                    out[r, f, :, 256:COLS] = value[:, :LAST]

    outer_lanes = (lane == jnp.where(polar, 63, 31)) | (lane == jnp.where(polar, 95, 127))

    def unpack(slot):
        row = lax.rem(slot + 1, ROWS + 2)
        got_west, got_east = from_west[slot], from_east[slot]
        for f in range(NF):
            own = jnp.where(lane < 2, tile(row, f, 0), fixed(tile(row, f, 2), 30 - (LAST - 1)))
            halo = jnp.where(lane >= 96, fixed(got_west, 96 - 32 * f), fixed(got_east, 31 - 32 * f))
            value = jnp.where(lane < 31, own, halo)
            if f != 1:
                outer = roll(x_both[(0, None, 1, 2)[f]], jnp.where(polar, 63, 127) - slot)
                value = jnp.where(outer_lanes, outer, value)
            edge[row, f] = value

    def late(r):
        row = r + 1
        width, keep, gain = coefficients(r)

        def difference(a):
            return roll(a, 127) - roll(a, 1)

        mids = [edge[row, f] for f in range(NF)]
        stepped = step(
            r, lambda f: mids[f], lambda f: edge[row + 1, f], lambda f: edge[row - 1, f],
            (difference(mids[0] * mids[2]), difference(mids[2]), difference(mids[3])),
        )
        right = weights(far, width)
        parts = [halves(a) for a in stepped]
        left = jnp.concatenate([jnp.concatenate(p, axis=1) for p in parts], axis=0)
        smooth = product(left, jnp.concatenate([right, right], axis=0))
        for f in range(NF):
            more = gain * smooth[f * LEV : (f + 1) * LEV, :128] + jnp.where(lane == 0, keep * stepped[f], 0.0)
            out[r, f, :, 0:128] = out[r, f, :, 0:128] + more
            last = roll(stepped[f], LAST - 1 - 30)
            more = gain * smooth[f * LEV : (f + 1) * LEV, 128:] + jnp.where(lane == LAST - 1, keep * last, 0.0)
            out[r, f, :, 256:COLS] = out[r, f, :, 256:COLS] + more[:, :LAST]

    def early_group(g, carry):
        for i in range(GROUP):
            early(lax.rem(g * GROUP + 1 + i, ROWS))
        return carry

    def late_group(g, carry):
        @pl.when(polar)
        def _():
            for side in range(2):
                chunk_copy(2 * g + 1, side).wait()
                chunk_copy(2 * g + 2, side).wait()

        for i in range(GROUP):
            unpack(g * GROUP + 2 + i)
            late(lax.rem(g * GROUP + 1 + i, ROWS))
        return carry

    def outer_rows():
        @pl.when(has_north)
        def _():
            row_copy(1, north).wait_recv()

        @pl.when(has_south)
        def _():
            row_copy(0, south).wait_recv()

        @pl.when(polar)
        def _():
            for i, row in enumerate((ROWS + 1, 0)):
                to_east[ROWS + i], to_west[ROWS + i] = pack(row, (1, 2, 3))
            for side in range(2):
                corner_copy(side).start()

    def crossing_send():
        @pl.when(last_south)
        def _():
            pl.semaphore_wait(ready.at[NORTH], 1)
            row_copy(0, north).start()

        @pl.when(first[SOUTH])
        def _():
            pl.semaphore_wait(ready.at[SOUTH], 1)
            row_copy(1, south).start()

    soon = polar & ~crossing & (lon == NLON_DEV - 1)

    def outer_early():
        for r in (ROWS - 1, 0):
            early(r)

    lax.fori_loop(0, 1, early_group, 0)
    send_stage(2)
    pl.when(lon < 2)(crossing_send)
    lax.fori_loop(1, 2, early_group, 0)
    send_stage(3)
    pl.when(soon)(outer_rows)
    pl.when(lon >= 2)(crossing_send)
    lax.fori_loop(2, 3, early_group, 0)
    send_stage(4)

    for r in range(3 * GROUP + 1, ROWS - 1):
        early(r)

    patient = crossing & (lon < NLON_DEV - 1)

    @pl.when(polar & ~patient)
    def _():
        pl.when(~soon)(outer_rows)
        outer_early()


    for side in range(2):
        x_copy(side).wait()
    near_x = jnp.where(polar, xf_east[...], xf_west[...])
    far_x = jnp.where(polar, xf_west[...], xf_east[...])
    for slot in range(3):
        x_both[slot] = jnp.where(lane < 32, fixed(near_x, -32 * slot), fixed(far_x, 32 - 32 * slot))

    @pl.when(polar)
    def _():
        for side in range(2):
            chunk_copy(0, side).wait()

    for slot in range(2):
        unpack(slot)
    lax.fori_loop(0, 1, late_group, 0)

    @pl.when(polar & patient)
    def _():
        outer_rows()
        outer_early()

    lax.fori_loop(1, 3, late_group, 0)

    @pl.when(polar)
    def _():
        for side in range(2):
            chunk_copy(NCHUNK - 1, side).wait()

    for r in range(3 * GROUP + 1, ROWS - 1):
        unpack(r + 1)
        late(r)

    @pl.when(~polar)
    def _():
        outer_rows()
        outer_early()

    @pl.when(polar)
    def _():
        for side in range(2):
            corner_copy(side).wait()

    unpack(ROWS)
    unpack(ROWS + 1)
    late(ROWS - 1)
    late(0)

    @pl.when(has_north)
    def _():
        row_copy(0, north).wait_send()

    @pl.when(has_south)
    def _():
        row_copy(1, south).wait_send()


def shards(state, band, damping):
    hbm = pl.BlockSpec(memory_space=pltpu.HBM)
    packed = pltpu.VMEM((ROWS + 2, LEV, 128), F32)
    extra = pltpu.VMEM((LEV, 128), F32)
    dma = pltpu.SemaphoreType.DMA
    return pl.pallas_call(
        kernel,
        out_shape=pltpu.VMEM(state.shape, F32),
        in_specs=[hbm] * 4,
        out_specs=pl.BlockSpec(memory_space=pltpu.VMEM),
        scratch_shapes=[
            pltpu.VMEM((ROWS + 2, NF, LEV, COLS), F32),
            packed, packed, packed, packed,
            extra, extra, extra, extra,
            pltpu.VMEM((3, LEV, 128), F32),
            pltpu.VMEM((ROWS + 2, NF, LEV, 128), F32),
            pltpu.VMEM((256, 128), BF16),
            pltpu.VMEM((128, 256), BF16),
            pltpu.SMEM((256,), jnp.int32),
            pltpu.SMEM((256,), F32),
            pltpu.SMEM((8, 128), F32),
            dma((NCHUNK,)), dma((3,)),
            dma((2, NCHUNK + 1)), dma((2, NCHUNK + 1)),
            dma((2,)), dma((2,)),
            dma((2,)), dma((2,)),
            pltpu.SemaphoreType.REGULAR((4,)),
        ],
        compiler_params=pltpu.CompilerParams(
            collective_id=0, has_side_effects=True, vmem_limit_bytes=60 * 1024 * 1024
        ),
    )(state, band, damping, jnp.asarray(row_table()))


def solution(mesh):
    in_specs = (P("lat", None, None, "lon"), P(), P())
    out_specs = P("lat", None, None, "lon")
    return jax.shard_map(shards, mesh=mesh, in_specs=in_specs, out_specs=out_specs, check_vma=False)
```

```python
import functools
import math

import jax
import jax.numpy as jnp
import numpy as np
from jax import lax
from jax.experimental import pallas as pl
from jax.experimental.pallas import tpu as pltpu
from jax.sharding import PartitionSpec as P

MAXB = 32
KX = 0.004
KY = 0.1
FC = 0.2

NLON_DEV = 8
NLAT_DEV = 16
NX = 4
ROWS = 32
NF = 4
LEV = 16
COLS = 360
LAST = COLS - 256
CHUNK = 4
NCHUNK = ROWS // CHUNK
STAGES = (3, 5, 7, 8)
GROUP = 8
MESH = pl.DeviceIdType.MESH
F32 = jnp.float32
BF16 = jnp.bfloat16


def row_table():
    total = ROWS * NLAT_DEV
    rows = np.arange(-1, total + 1, dtype=np.float32)
    angle = np.float32(math.pi) * ((rows + np.float32(0.5)) / np.float32(total) - np.float32(0.5))
    cos = np.cos(angle.astype(np.float64)).astype(np.float32)
    sin = np.sin(angle.astype(np.float64)).astype(np.float32)
    inv = np.float32(1.0) / cos
    table = np.zeros((NLAT_DEV, 8, 128), np.float32)
    for lat in range(NLAT_DEV):
        pad = slice(lat * ROWS, lat * ROWS + ROWS + 2)
        mid = slice(lat * ROWS + 1, lat * ROWS + ROWS + 1)
        table[lat, 0, : ROWS + 2] = cos[pad]
        table[lat, 1, :ROWS] = np.float32(KX) * inv[mid]
        table[lat, 2, :ROWS] = np.float32(KY) * inv[mid]
        table[lat, 3, :ROWS] = np.float32(FC) * sin[mid]
    return table


def kernel(
    state, band_hbm, damping_hbm, table_hbm, out,
    buf, to_east, to_west, from_west, from_east, x_east, x_west, xf_west, xf_east, x_both,
    edge, near, far, band, damping, table,
    load_sem, small_sem, send_sem, recv_sem, row_send, row_recv, x_send, x_recv, ready,
):
    lon, lat = lax.axis_index("lon"), lax.axis_index("lat")
    east, west = lax.rem(lon + 1, NLON_DEV), lax.rem(lon + NLON_DEV - 1, NLON_DEV)
    north, south = lax.rem(lat + 1, NLAT_DEV), lax.rem(lat + NLAT_DEV - 1, NLAT_DEV)
    has_north, has_south = lat < NLAT_DEV - 1, lat > 0
    x = lax.rem(lat, NX)
    polar = (lat < NLAT_DEV // 4) | (lat >= NLAT_DEV - NLAT_DEV // 4)
    crossing = ((x == NX - 1) & has_north) | ((x == 0) & has_south)
    last_south, first_mid = lat == NLAT_DEV // 4 - 1, lat == NLAT_DEV // 4
    first = ((x < NX - 1) | last_south, (x == 0) & has_south & ~first_mid, lon < NLON_DEV - 1, lon == 0)
    second = ((x == NX - 1) & has_north & ~last_south, (x > 0) | first_mid, lon == NLON_DEV - 1, lon > 0)
    others = ((lon, north), (lon, south), (east, lat), (west, lat))
    NORTH, SOUTH, EAST, WEST = range(4)
    OPPOSITE = (SOUTH, NORTH, WEST, EAST)

    def at(a, b):
        return {"lon": a, "lat": b}

    def load(c):
        rows = pl.ds(c * CHUNK, CHUNK)
        return pltpu.make_async_copy(
            state.at[rows], buf.at[pl.ds(c * CHUNK + 1, CHUNK)], load_sem.at[c]
        )

    smalls = [
        pltpu.make_async_copy(band_hbm, band, small_sem.at[0]),
        pltpu.make_async_copy(damping_hbm, damping, small_sem.at[1]),
        pltpu.make_async_copy(table_hbm.at[lat], table, small_sem.at[2]),
    ]
    for c in range(NCHUNK):
        load(c).start()
    for copy in smalls:
        copy.start()

    barrier = pltpu.get_barrier_semaphore()
    for side in range(4):

        @pl.when(first[side])
        def _():
            pl.semaphore_signal(barrier, 1, device_id=at(*others[side]), device_id_type=MESH)

    @pl.when(lon == 1)
    def _():
        pl.semaphore_signal(barrier, 1, device_id=at(west, lat), device_id_type=MESH)

    k = lax.broadcasted_iota(jnp.int32, (256, 128), 0)
    n = lax.broadcasted_iota(jnp.int32, (256, 128), 1)
    place = jnp.where(k < 192, k, k - 256)
    near[...] = jnp.minimum(jnp.abs(place - n), 255).astype(F32).astype(BF16)
    k = lax.broadcasted_iota(jnp.int32, (128, 256), 0)
    n = lax.broadcasted_iota(jnp.int32, (128, 256), 1)
    place = jnp.where(k >= 96, k - 128, jnp.where(k == 0, 0, jnp.where((k >= 30) & (k < 63), k + 329, 10000)))
    column = jnp.where(n < 128, n, n + 128)
    far[...] = jnp.minimum(jnp.abs(place - column), 255).astype(F32).astype(BF16)

    @pl.when(~has_south)
    def _():
        buf[0, 1:4] = jnp.zeros((3, LEV, COLS), F32)

    @pl.when(~has_north)
    def _():
        buf[ROWS + 1, 1:4] = jnp.zeros((3, LEV, COLS), F32)

    @pl.when(~polar)
    def _():
        from_west[...] = jnp.zeros(from_west.shape, F32)
        from_east[...] = jnp.zeros(from_east.shape, F32)

    pl.semaphore_wait(barrier, sum(jnp.where(flag, 1, 0) for flag in (*second, lon == 0)))

    def row_copy(i, target):
        source = state.at[ROWS - 1 if i == 0 else 0, pl.ds(1, 3)]
        goal = buf.at[0 if i == 0 else ROWS + 1, pl.ds(1, 3)]
        return pltpu.make_async_remote_copy(
            source, goal, row_send.at[i], row_recv.at[i], device_id=at(lon, target), device_id_type=MESH
        )

    @pl.when(second[SOUTH])
    def _():
        row_copy(1, south).start()

    @pl.when(second[NORTH])
    def _():
        row_copy(0, north).start()

    for side in range(4):

        @pl.when(second[side])
        def _():
            pl.semaphore_signal(ready.at[OPPOSITE[side]], 1, device_id=at(*others[side]), device_id_type=MESH)

    lane = lax.broadcasted_iota(jnp.int32, (LEV, 128), 1)

    def tile(row, field, t):
        if t < 2:
            return buf[row, field, :, t * 128 : (t + 1) * 128]
        return jnp.concatenate([buf[row, field, :, 256:COLS], jnp.zeros((LEV, 128 - LAST), F32)], axis=1)

    def roll(a, shift):
        return pltpu.roll(a, shift, 1)

    def fixed(a, shift):
        return a if shift % 128 == 0 else pltpu.roll(a, shift % 128, 1)

    def pack(row, fields=range(NF)):
        for_east = jnp.zeros((LEV, 128), F32)
        for_west = jnp.zeros((LEV, 128), F32)
        for f in fields:
            here = (lane >= 32 * f) & (lane < 32 * f + 32)
            for_east = jnp.where(here, fixed(tile(row, f, 2), 32 * f - (LAST - 32)), for_east)
            for_west = jnp.where(here, fixed(tile(row, f, 0), 32 * f), for_west)
        return for_east, for_west

    def chunk_copy(c, i):
        source, goal, target = ((to_east, from_west, east), (to_west, from_east, west))[i]
        rows = pl.ds(c * CHUNK, CHUNK)
        return pltpu.make_async_remote_copy(
            source.at[rows], goal.at[rows], send_sem.at[i, c], recv_sem.at[i, c],
            device_id=at(target, lat), device_id_type=MESH,
        )

    def corner_copy(i):
        source, goal, target = ((to_east, from_west, east), (to_west, from_east, west))[i]
        rows = pl.ds(ROWS, 2)
        return pltpu.make_async_remote_copy(
            source.at[rows], goal.at[rows], send_sem.at[i, NCHUNK], recv_sem.at[i, NCHUNK],
            device_id=at(target, lat), device_id_type=MESH,
        )

    def x_copy(side):
        source, goal, target = ((x_east, xf_west, east), (x_west, xf_east, west))[side]
        return pltpu.make_async_remote_copy(
            source, goal, x_send.at[side], x_recv.at[side], device_id=at(target, lat), device_id_type=MESH
        )

    def pack_chunk(c, carry):
        xe, xw = carry
        load(c).wait()
        for i in range(CHUNK):
            r = c * CHUNK + i
            to_east[r], to_west[r] = pack(r + 1)
            for slot, f in enumerate((0, 2, 3)):
                goal = 32 * slot + r
                here = lane == goal
                xe = jnp.where(here, roll(tile(r + 1, f, 2), lax.rem(goal + 256 - jnp.where(polar, LAST - 33, LAST - 1), 128)), xe)
                xw = jnp.where(here, roll(tile(r + 1, f, 0), lax.rem(goal + 256 - jnp.where(polar, 32, 0), 128)), xw)

        early_chunk = polar & (c < STAGES[0])

        @pl.when(early_chunk & second[EAST])
        def _():
            chunk_copy(c, 0).start()

        @pl.when(early_chunk & second[WEST])
        def _():
            chunk_copy(c, 1).start()

        return xe, xw

    xe, xw = lax.fori_loop(0, NCHUNK, pack_chunk, (jnp.zeros((LEV, 128), F32),) * 2)
    x_east[...] = xe
    x_west[...] = xw

    def send_stage(stage):
        ends = (0, *STAGES, NCHUNK)
        for i in range(2):
            is_first = first[(EAST, WEST)[i]]
            begin = jnp.where(is_first, ends[stage - 1], ends[stage])
            end = jnp.where(polar, jnp.where(is_first, ends[stage], ends[stage + 1]), begin)

            def send(c, carry):
                chunk_copy(c, i).start()
                return carry

            lax.fori_loop(begin, end, send, 0)

    @pl.when(first[EAST])
    def _():
        pl.semaphore_wait(ready.at[EAST], 1)

    x_copy(0).start()

    @pl.when(first[NORTH] & ~last_south)
    def _():
        pl.semaphore_wait(ready.at[NORTH], 1)
        row_copy(0, north).start()

    @pl.when(first[WEST])
    def _():
        pl.semaphore_wait(ready.at[WEST], 1)

    x_copy(1).start()
    send_stage(1)
    for copy in smalls:
        copy.wait()

    origin = jnp.where(lat < NLAT_DEV // 4, lat * ROWS, jnp.where(polar, lat * ROWS - 256, 0))

    def coefficients(r):
        width = jnp.full((LEV, 128), band[origin + r], jnp.int32).astype(F32) + 1.0
        strength = jnp.full((LEV, 128), jnp.where(polar, damping[origin + r], 0.0), F32)
        return width, 1.0 - strength, strength / (width * width)

    def weights(distances, width):
        top = width.astype(BF16)
        rows, columns = distances.shape
        top = jnp.concatenate([top] * (rows // LEV), axis=0)
        top = jnp.concatenate([top] * (columns // 128), axis=1)
        return jnp.maximum(top - distances[...], jnp.zeros((), BF16))

    def step(r, mid, up, down, diff):
        kx, ky, fs = table[1, r], table[2, r], table[3, r]
        u, v, h, q = (mid(f) for f in range(NF))
        vn, hn, qn = (up(f) for f in (1, 2, 3))
        vs, hs, qs = (down(f) for f in (1, 2, 3))
        flux = vn * hn * table[0, r + 2] - vs * hs * table[0, r]
        d_flux, d_h, d_q = diff
        h_new = h - kx * d_flux - ky * flux
        u_new = u - kx * d_h + fs * v
        v_new = v - KY * (hn - hs) - fs * u
        q_new = q - kx * u * d_q - KY * v * (qn - qs)
        return u_new, v_new, h_new, q_new

    def halves(a):
        high = a.astype(BF16)
        return high, (a - high.astype(F32)).astype(BF16)

    def product(left, right):
        return jnp.dot(left, right, preferred_element_type=F32)

    def early(r, filtered=True):
        row = r + 1
        width, keep, gain = coefficients(r)
        mids = [[tile(row, f, t) for t in range(3)] for f in range(NF)]

        def difference(tiles):
            lo = [roll(a, 127) for a in tiles]
            hi = [roll(a, 1) for a in tiles]
            result = []
            for t in range(3):
                e = lo[t] if t == 2 else jnp.where(lane == 127, lo[t + 1], lo[t])
                w = hi[t] if t == 0 else jnp.where(lane == 0, hi[t - 1], hi[t])
                result.append(e - w)
            return result

        d_flux = difference([mids[0][t] * mids[2][t] for t in range(3)])
        d_h = difference(mids[2])
        d_q = difference(mids[3])
        stepped = []
        for t in range(3):
            values = step(
                r, lambda f: mids[f][t], lambda f: tile(row + 1, f, t), lambda f: tile(row - 1, f, t),
                (d_flux[t], d_h[t], d_q[t]),
            )
            if t == 0:
                values = [jnp.where(lane == 0, 0.0, a) for a in values]
            if t == 2:
                values = [jnp.where(lane >= LAST - 1, 0.0, a) for a in values]
            stepped.append(values)
        if not filtered:
            for t in range(3):
                for f in range(NF):
                    if t < 2:
                        out[r, f, :, t * 128 : (t + 1) * 128] = stepped[t][f]
                    else:
                        out[r, f, :, 256:COLS] = stepped[t][f][:, :LAST]
            return
        right = weights(near, width)
        parts = [[halves(a) for a in values] for values in stepped]
        zero = jnp.zeros((LEV, 128), BF16)

        def left(half):
            blocks = []
            for t in range(3):
                for f in range(NF):
                    after = parts[t + 1][f][half] if t < 2 else zero
                    before = parts[t - 1][f][half] if t > 0 else zero
                    side = jnp.where(lane < 64, after, before)
                    blocks.append(jnp.concatenate([parts[t][f][half], side], axis=1))
            return jnp.concatenate(blocks, axis=0)

        both = product(jnp.concatenate([left(0), left(1)], axis=0), right)
        smooth = both[: both.shape[0] // 2] + both[both.shape[0] // 2 :]
        for t in range(3):
            for f in range(NF):
                place = (t * NF + f) * LEV
                value = keep * stepped[t][f] + gain * smooth[place : place + LEV]
                if t < 2:
                    out[r, f, :, t * 128 : (t + 1) * 128] = value
                else:
                    out[r, f, :, 256:COLS] = value[:, :LAST]

    outer_lanes = (lane == jnp.where(polar, 63, 31)) | (lane == jnp.where(polar, 95, 127))

    def unpack(slot):
        row = lax.rem(slot + 1, ROWS + 2)
        got_west, got_east = from_west[slot], from_east[slot]
        for f in range(NF):
            own = jnp.where(lane < 2, tile(row, f, 0), fixed(tile(row, f, 2), 30 - (LAST - 1)))
            halo = jnp.where(lane >= 96, fixed(got_west, 96 - 32 * f), fixed(got_east, 31 - 32 * f))
            value = jnp.where(lane < 31, own, halo)
            if f != 1:
                outer = roll(x_both[(0, None, 1, 2)[f]], jnp.where(polar, 63, 127) - slot)
                value = jnp.where(outer_lanes, outer, value)
            edge[row, f] = value

    def late(r, filtered=True):
        row = r + 1
        width, keep, gain = coefficients(r)

        def difference(a):
            return roll(a, 127) - roll(a, 1)

        mids = [edge[row, f] for f in range(NF)]
        stepped = step(
            r, lambda f: mids[f], lambda f: edge[row + 1, f], lambda f: edge[row - 1, f],
            (difference(mids[0] * mids[2]), difference(mids[2]), difference(mids[3])),
        )
        if not filtered:
            for f in range(NF):
                out[r, f, :, 0:128] = jnp.where(lane == 0, stepped[f], out[r, f, :, 0:128])
                last = roll(stepped[f], LAST - 1 - 30)[:, :LAST]
                out[r, f, :, 256:COLS] = jnp.where(lane[:, :LAST] == LAST - 1, last, out[r, f, :, 256:COLS])
            return
        right = weights(far, width)
        parts = [halves(a) for a in stepped]
        left = jnp.concatenate([jnp.concatenate(p, axis=1) for p in parts], axis=0)
        smooth = product(left, jnp.concatenate([right, right], axis=0))
        for f in range(NF):
            more = gain * smooth[f * LEV : (f + 1) * LEV, :128] + jnp.where(lane == 0, keep * stepped[f], 0.0)
            out[r, f, :, 0:128] = out[r, f, :, 0:128] + more
            last = roll(stepped[f], LAST - 1 - 30)
            more = gain * smooth[f * LEV : (f + 1) * LEV, 128:] + jnp.where(lane == LAST - 1, keep * last, 0.0)
            out[r, f, :, 256:COLS] = out[r, f, :, 256:COLS] + more[:, :LAST]

    def early_group(g, carry):
        for i in range(GROUP):
            early(lax.rem(g * GROUP + 1 + i, ROWS))
        return carry

    def late_group(g, carry):
        @pl.when(polar)
        def _():
            for side in range(2):
                chunk_copy(2 * g + 1, side).wait()
                chunk_copy(2 * g + 2, side).wait()

        for i in range(GROUP):
            unpack(g * GROUP + 2 + i)
            late(lax.rem(g * GROUP + 1 + i, ROWS))
        return carry

    def outer_rows():
        @pl.when(has_north)
        def _():
            row_copy(1, north).wait_recv()

        @pl.when(has_south)
        def _():
            row_copy(0, south).wait_recv()

        @pl.when(polar)
        def _():
            for i, row in enumerate((ROWS + 1, 0)):
                to_east[ROWS + i], to_west[ROWS + i] = pack(row, (1, 2, 3))
            for side in range(2):
                corner_copy(side).start()

    def crossing_send():
        @pl.when(last_south)
        def _():
            pl.semaphore_wait(ready.at[NORTH], 1)
            row_copy(0, north).start()

        @pl.when(first[SOUTH])
        def _():
            pl.semaphore_wait(ready.at[SOUTH], 1)
            row_copy(1, south).start()

    soon = polar & ~crossing & (lon == NLON_DEV - 1)

    def outer_early():
        for r in (ROWS - 1, 0):
            early(r)

    lax.fori_loop(0, 1, early_group, 0)
    send_stage(2)
    pl.when(lon < 2)(crossing_send)
    lax.fori_loop(1, 2, early_group, 0)
    send_stage(3)
    pl.when(soon)(outer_rows)
    pl.when(lon >= 2)(crossing_send)
    lax.fori_loop(2, 3, early_group, 0)
    send_stage(4)

    for r in range(3 * GROUP + 1, ROWS - 1):
        early(r)

    patient = crossing & (lon < NLON_DEV - 1)

    @pl.when(polar & ~patient)
    def _():
        pl.when(~soon)(outer_rows)
        outer_early()


    for side in range(2):
        x_copy(side).wait()
    near_x = jnp.where(polar, xf_east[...], xf_west[...])
    far_x = jnp.where(polar, xf_west[...], xf_east[...])
    for slot in range(3):
        x_both[slot] = jnp.where(lane < 32, fixed(near_x, -32 * slot), fixed(far_x, 32 - 32 * slot))

    @pl.when(polar)
    def _():
        for side in range(2):
            chunk_copy(0, side).wait()

    for slot in range(2):
        unpack(slot)
    lax.fori_loop(0, 1, late_group, 0)

    @pl.when(polar & patient)
    def _():
        outer_rows()
        outer_early()

    lax.fori_loop(1, 3, late_group, 0)

    @pl.when(polar)
    def _():
        for side in range(2):
            chunk_copy(NCHUNK - 1, side).wait()

    for r in range(3 * GROUP + 1, ROWS - 1):
        unpack(r + 1)
        late(r)

    def outer_late(filtered):
        unpack(ROWS)
        unpack(ROWS + 1)
        late(ROWS - 1, filtered)
        late(0, filtered)

    @pl.when(~polar)
    def _():
        outer_rows()
        for r in (ROWS - 1, 0):
            early(r, False)
        outer_late(False)

    @pl.when(polar)
    def _():
        for side in range(2):
            corner_copy(side).wait()
        outer_late(True)

    @pl.when(has_north)
    def _():
        row_copy(0, north).wait_send()

    @pl.when(has_south)
    def _():
        row_copy(1, south).wait_send()


def shards(state, band, damping):
    hbm = pl.BlockSpec(memory_space=pltpu.HBM)
    packed = pltpu.VMEM((ROWS + 2, LEV, 128), F32)
    extra = pltpu.VMEM((LEV, 128), F32)
    dma = pltpu.SemaphoreType.DMA
    return pl.pallas_call(
        kernel,
        out_shape=pltpu.VMEM(state.shape, F32),
        in_specs=[hbm] * 4,
        out_specs=pl.BlockSpec(memory_space=pltpu.VMEM),
        scratch_shapes=[
            pltpu.VMEM((ROWS + 2, NF, LEV, COLS), F32),
            packed, packed, packed, packed,
            extra, extra, extra, extra,
            pltpu.VMEM((3, LEV, 128), F32),
            pltpu.VMEM((ROWS + 2, NF, LEV, 128), F32),
            pltpu.VMEM((256, 128), BF16),
            pltpu.VMEM((128, 256), BF16),
            pltpu.SMEM((256,), jnp.int32),
            pltpu.SMEM((256,), F32),
            pltpu.SMEM((8, 128), F32),
            dma((NCHUNK,)), dma((3,)),
            dma((2, NCHUNK + 1)), dma((2, NCHUNK + 1)),
            dma((2,)), dma((2,)),
            dma((2,)), dma((2,)),
            pltpu.SemaphoreType.REGULAR((4,)),
        ],
        compiler_params=pltpu.CompilerParams(
            collective_id=0, has_side_effects=True, vmem_limit_bytes=60 * 1024 * 1024
        ),
    )(state, band, damping, jnp.asarray(row_table()))


def solution(mesh):
    in_specs = (P("lat", None, None, "lon"), P(), P())
    out_specs = P("lat", None, None, "lon")
    return jax.shard_map(shards, mesh=mesh, in_specs=in_specs, out_specs=out_specs, check_vma=False)
```
